1024 devices in a mesh: dp: 16 (over z, core), expert: 64 (over y, x).
Axes of the slice: x: 8, y: 8, z: 8, core: 2. Of those that a mesh axis runs over, the one named last changes fastest.
Arguments:
- tokens: bfloat16 [1024, 4096], P(('expert', 'dp')), may hold values from -6 to 6
- expert_ids: int32 [1024, 8], P('expert'), may hold values from 0 to 63, all different within a row; in each aligned block of 16 rows (0 to 15, 16 to 31, ...) at most 3 rows name the same one
- gates: float32 [1024, 8], P('expert'), may hold values from 0.05 to 0.5
- w_gate: bfloat16 [64, 1024, 4096], P('expert', 'dp'), may hold values from -0.09375 to 0.09375
- w_up: bfloat16 [64, 1024, 4096], P('expert', 'dp'), may hold values from -0.09375 to 0.09375
- w_down: bfloat16 [64, 1024, 4096], P('expert', 'dp'), may hold values from -0.1875 to 0.1875
- cotangent: bfloat16 [1024, 4096], P(('expert', 'dp')), may hold values from -0.75 to 0.75
Outputs:
- mixed: bfloat16 [1024, 4096], P(('expert', 'dp'))
- token_grad: bfloat16 [1024, 4096], P(('expert', 'dp'))
- gate_grad: float32 [1024, 8], P(('expert', 'dp'))
- w_gate_grad: bfloat16 [64, 1024, 4096], P('expert', 'dp')
- w_up_grad: bfloat16 [64, 1024, 4096], P('expert', 'dp')
- w_down_grad: bfloat16 [64, 1024, 4096], P('expert', 'dp')
The draws below stay inside these ranges and needn't reach their ends.
Inputs may be any that keep to these rules, and one draw needn't show every extreme that they name: `expert_ids`: each token names 8 different experts. Among the 16 tokens of one index of the expert axis (aligned blocks of rows) no expert is named more than 3 times, and in every draw some expert is named exactly 3 times in some block.
All inputs are finite; a program needn't handle non-finite values.
Results may differ from the reference program's by a relative error of at most 0.0075.
Values may be sent and summed in bfloat16 or wider, within the bound.
A program may use at most 32 MiB of HBM per device.

```python
import math
import jax
import jax.numpy as jnp
import numpy as np
from jax import lax

D = 4096
FF = 1024
TOPK = 8
TOK_DEV = 16
EXPERTS = 64
TOKENS = 1024
CAP = 3
N_DP = 16
N_EXPERT = 64


def block_levels(own_key, extent, split, smallest, top_value):
    level, own = 1.0, jax.random.fold_in(own_key, 6)
    for dim, parts in split:
        steps = jnp.exp(jax.random.uniform(jax.random.fold_in(own, dim), (parts,), jnp.float32, smallest / len(split), top_value / len(split)))
        level = level * jnp.repeat(steps, extent[dim] // parts).reshape([-1 if axis == dim else 1 for axis in range(len(extent))])
    return level


def deal_out(stream_key, own, number, rows, amount, top, bound, lean):
    ranking = jax.random.permutation(stream_key, amount)
    packed, ordinary = portions_of(amount, rows * top, bound, lean, True), portions_of(amount, rows * top, bound, lean, False)
    places = jnp.arange(amount)

    def named(tallies, turn):
        used = int((tallies > 0).sum())
        fixed = max(1, used // 4)
        moved = fixed + (places - fixed + turn * (used - fixed)) % max(1, amount - fixed)
        return jnp.zeros((amount,), jnp.int32).at[ranking[jnp.where(places < fixed, places, moved)]].set(jnp.asarray(tallies, jnp.int32))

    tallies = jnp.where(number % 4 == 0, named(packed, number // 4), named(ordinary, number - number // 4 - 1))
    mixed = jax.random.permutation(jax.random.fold_in(own, 3), amount)
    giver, receiver = mixed[0:amount // 2 * 2:2], mixed[1:amount // 2 * 2:2]
    slack = jnp.minimum(tallies[giver] - 1, bound - tallies[receiver]) // 2
    slack = jnp.where((giver == ranking[0]) | (receiver == ranking[0]) | (tallies[receiver] == 0), 0, jnp.maximum(slack, 0))
    moved = jax.random.randint(jax.random.fold_in(own, 4), (amount // 2,), 0, 1 << 20) % (slack + 1)
    tallies = tallies.at[giver].add(-moved).at[receiver].add(moved)
    labels = jnp.searchsorted(jnp.cumsum(tallies), jnp.arange(rows * top), side="right").astype(jnp.int32)
    table = labels.reshape(top, rows).T
    table = table[jax.random.permutation(jax.random.fold_in(own, 1), rows)]
    turn = jax.random.randint(jax.random.fold_in(own, 2), (rows, 1), 0, top)
    return jnp.take_along_axis(table, (jnp.arange(top)[None, :] + turn) % top, axis=1)


def portions_of(amount, total, limit, lean, full):
    weights = [(1 << 20) // math.isqrt(standing ** lean) + 1 for standing in range(1, amount + 1)]
    largest = limit if full else min(limit, max(-(-total // amount), total * weights[0] // sum(weights)))
    least = 1 if total - largest >= amount - 1 else 0
    holding, surplus = [largest] + [least] * (amount - 1), total - largest - least * (amount - 1)
    while surplus > 0:
        free = [i for i in range(1, amount) if holding[i] < largest] or [i for i in range(1, amount) if holding[i] < limit]
        pool, remaining = sum([weights[i] for i in free]), surplus
        for i in free:
            extra = min(limit - holding[i], max(1, remaining * weights[i] // pool), surplus)
            holding[i] = holding[i] + extra
            surplus = surplus - extra
    return np.array(holding)


def gaussian(stream_key, dims, scale, limit, cuts=(), kind=jnp.bfloat16):
    gain = block_levels(stream_key, dims, cuts, -0.22, 0.18) if cuts else 1.0
    array = jax.random.normal(stream_key, dims, jnp.float32) * scale * gain
    return jnp.minimum(jnp.maximum(array, -limit), limit).astype(kind)


def setup_inputs(seed: int = 0) -> dict:
    key_list = jax.random.split(jax.random.key(seed), 8)
    tokens = gaussian(key_list[0], (TOKENS, D), 1.0, 6.0, ((0, 1024),))
    expert_ids_keys = jax.random.split(jax.random.fold_in(key_list[1], 1), TOKENS // TOK_DEV)
    expert_ids_turns = jax.random.permutation(jax.random.fold_in(key_list[1], 3), TOKENS // TOK_DEV)
    expert_ids = jax.vmap(lambda own, number: deal_out(jax.random.fold_in(key_list[1], 2), own, number, TOK_DEV, EXPERTS, TOPK, CAP, 2))(expert_ids_keys, expert_ids_turns).reshape((TOKENS, TOPK))
    gates = jnp.clip(0.05 + 0.45 * jax.random.uniform(key_list[2], (TOKENS, TOPK), jnp.float32) ** block_levels(key_list[2], (TOKENS, TOPK), ((0, 64),), -0.2, 0.2), 0.05, 0.5)
    w_gate = gaussian(key_list[3], (EXPERTS, FF, D), D ** -0.5, 0.09375, ((0, 64), (1, 16)))
    w_up = gaussian(key_list[4], (EXPERTS, FF, D), D ** -0.5, 0.09375, ((0, 64), (1, 16)))
    w_down = gaussian(key_list[5], (EXPERTS, FF, D), FF ** -0.5, 0.1875, ((0, 64), (1, 16)))
    cotangent = gaussian(key_list[6], (TOKENS, D), 0.125, 0.75, ((0, 1024),))
    return {"tokens": tokens, "expert_ids": expert_ids, "gates": gates, "w_gate": w_gate, "w_up": w_up, "w_down": w_down, "cotangent": cotangent}


def contract(left, right, left_dim, right_dim):
    return lax.dot_general(left, right, (((left_dim,), (right_dim,)), ((), ())), preferred_element_type=jnp.float32)


def reference(tokens, expert_ids, gates, w_gate, w_up, w_down, cotangent):
    slots = N_EXPERT * CAP
    total = tokens.shape[0]
    width = tokens.shape[1]
    hidden_units = w_gate.shape[1]
    block = hidden_units // N_DP
    order = jnp.arange(total, dtype=jnp.int32)

    def per_expert(carry, inputs):
        out_sum, grad_sum, gate_sum = carry
        weight_gate, weight_up, weight_down, expert = inputs
        picked = expert_ids == expert
        member = jnp.any(picked, axis=1).astype(jnp.int32)
        gate_of = jnp.sum(jnp.where(picked, gates, jnp.zeros_like(gates)), axis=1)
        position = jnp.where(member > 0, jnp.cumsum(member) - 1, slots).astype(jnp.int32)
        source = jnp.zeros((slots,), jnp.int32).at[position].set(order, mode="drop")
        filled = jnp.zeros((slots,), jnp.float32).at[position].set(1.0, mode="drop")
        arrived = tokens[source] * filled.astype(jnp.bfloat16)[:, None]
        grad_rows = cotangent[source]
        slot_gate = gate_of[source] * filled
        gate_pre = contract(arrived, weight_gate, 1, 1)
        up_pre = contract(arrived, weight_up, 1, 1)
        hidden = (jax.nn.silu(gate_pre) * up_pre).astype(jnp.bfloat16)
        pieces = jnp.einsum("sgf,gfd->gsd", hidden.reshape(slots, N_DP, block).astype(jnp.float32),
                            weight_down.reshape(N_DP, block, width).astype(jnp.float32))
        rounded = lax.optimization_barrier(pieces.astype(jnp.bfloat16))
        expert_out = jnp.sum(rounded.astype(jnp.float32), axis=0)
        out_sum = out_sum.at[source].add(slot_gate[:, None] * expert_out)
        scores = jnp.sum(grad_rows.astype(jnp.float32) * expert_out, axis=1)
        scores_ext = jnp.concatenate([scores, jnp.zeros((1,), scores.dtype)])
        gate_sum = gate_sum + jnp.where(picked, scores_ext[position][:, None], jnp.zeros_like(gate_sum))
        out_grad = (slot_gate[:, None] * grad_rows.astype(jnp.float32)).astype(jnp.bfloat16)
        down_grad = contract(hidden, out_grad, 0, 0)
        hidden_grad = contract(out_grad, weight_down, 1, 1)
        logistic = jax.nn.sigmoid(gate_pre)
        act_gate = (hidden_grad * up_pre * logistic * (1.0 + gate_pre * (1.0 - logistic))).astype(jnp.bfloat16)
        act_up = (hidden_grad * gate_pre * logistic).astype(jnp.bfloat16)
        gate_wgrad = contract(act_gate, arrived, 0, 0)
        up_wgrad = contract(act_up, arrived, 0, 0)
        back = jnp.einsum("sgf,gfd->gsd", act_gate.reshape(slots, N_DP, block).astype(jnp.float32),
                          weight_gate.reshape(N_DP, block, width).astype(jnp.float32))
        back = back + jnp.einsum("sgf,gfd->gsd", act_up.reshape(slots, N_DP, block).astype(jnp.float32),
                                 weight_up.reshape(N_DP, block, width).astype(jnp.float32))
        back_rounded = lax.optimization_barrier(back.astype(jnp.bfloat16))
        input_part = jnp.sum(back_rounded.astype(jnp.float32), axis=0)
        grad_sum = grad_sum.at[source].add(input_part)
        return (out_sum, grad_sum, gate_sum), (gate_wgrad.astype(jnp.bfloat16), up_wgrad.astype(jnp.bfloat16), down_grad.astype(jnp.bfloat16))

    start = (jnp.zeros((total, width), jnp.float32), jnp.zeros((total, width), jnp.float32),
             jnp.zeros(gates.shape, jnp.float32))
    experts_all = jnp.arange(w_gate.shape[0], dtype=jnp.int32)
    (out_sum, grad_sum, gate_sum), (gate_grads, up_grads, down_grads) = lax.scan(
        per_expert, start, (w_gate, w_up, w_down, experts_all))
    return (out_sum.astype(jnp.bfloat16), grad_sum.astype(jnp.bfloat16), gate_sum, gate_grads, up_grads, down_grads)
```

```python
import functools

import jax
import jax.numpy as jnp
from jax import lax
from jax.experimental import pallas as pl
from jax.experimental.pallas import tpu as pltpu
from jax.sharding import PartitionSpec as P

F32 = jnp.float32
BF16 = jnp.bfloat16
MESH = pl.DeviceIdType.MESH
SLOTS = 3
LANES = 128
Q = 8
J = 16
GROUP = 16
HIGH = lax.Precision.HIGHEST


def mm(left, right, left_dim=1, right_dim=0, precision=None):
    return lax.dot_general(
        left,
        right,
        (((left_dim,), (right_dim,)), ((), ())),
        preferred_element_type=F32,
        precision=precision,
    )


def iota(shape, dim):
    return lax.broadcasted_iota(jnp.int32, shape, dim)


def split2(value):
    high = value.astype(BF16)
    return high, (value - high.astype(F32)).astype(BF16)


def kernel(
    ndp,
    nexp,
    tok_ref,
    cot_ref,
    ids_ref,
    gates_ref,
    wg_ref,
    wu_ref,
    wd_ref,
    mixed_ref,
    tgrad_ref,
    ggrad_ref,
    wgg_ref,
    wug_ref,
    wdg_ref,
    wgu,
    wd,
    gu_out,
    d_out,
    send_a,
    recv_a,
    send_b,
    recv_b,
    gath,
    part,
    sib_rx,
    ring_tx,
    ring_rx,
    send_c,
    recv_c,
    send_d,
    recv_d,
    pd_hi,
    pd_lo,
    pr_hi,
    pr_lo,
    score_mask,
    vcol,
    w_sem,
    o_sem,
    a_sem,
    b_sem,
    c_sem,
    d_sem,
    ag_send,
    ag_recv,
    sibg_send,
    sibg_recv,
    own_sem,
    sibr_send,
    sibr_recv,
    rs_send,
    rs_recv,
):
    g = lax.axis_index("dp")
    e = lax.axis_index("expert")
    nz = ndp // 2
    far = nz // 2
    z = g // 2
    core = lax.rem(g, 2)
    other = 1 - core
    rows = SLOTS * nexp
    half_rows = rows // 2
    ff = wd.shape[0]
    ncol = ndp * Q
    ds = 2 * LANES
    top = ids_ref.shape[1]

    def at_z(offset, which):
        return lax.rem(z + offset + nz, nz) * 2 + which

    right = at_z(1, core)
    left = at_z(-1, core)
    sibling = z * 2 + other
    toward = (right, left)

    barrier = pltpu.get_barrier_semaphore()

    def greet_dp(i, carry):
        pl.semaphore_signal(
            barrier, inc=1, device_id=(lax.rem(g + i, ndp), e), device_id_type=MESH
        )
        return carry

    def greet_expert(i, carry):
        pl.semaphore_signal(
            barrier, inc=1, device_id=(g, lax.rem(e + i, nexp)), device_id_type=MESH
        )
        return carry

    lax.fori_loop(1, ndp, greet_dp, 0)
    lax.fori_loop(1, nexp, greet_expert, 0)

    loads = [
        pltpu.make_async_copy(wg_ref.at[0], wgu.at[pl.ds(0, ff)], w_sem.at[0]),
        pltpu.make_async_copy(wu_ref.at[0], wgu.at[pl.ds(ff, ff)], w_sem.at[1]),
        pltpu.make_async_copy(wd_ref.at[0], wd, w_sem.at[2]),
    ]
    for load in loads:
        load.start()

    token = tok_ref[...].astype(F32)
    cotan = cot_ref[...].astype(F32)
    send_a[...] = jnp.zeros(send_a.shape, F32)
    for to in range(ndp):
        for half in range(2):
            lane = to * ds + half * LANES
            send_a[to, half : half + 1, :] = token[:, lane : lane + LANES]
            send_a[to, 2 + half : 3 + half, :] = cotan[:, lane : lane + LANES]

    pl.semaphore_wait(barrier, ndp - 1 + nexp - 1)

    def exchange(src, dst, sem, count, me, peer_id):
        def start(i, carry):
            peer = lax.rem(me + i, count)
            pltpu.make_async_remote_copy(
                src_ref=src.at[peer],
                dst_ref=dst.at[me],
                send_sem=sem.at[0],
                recv_sem=sem.at[1],
                device_id=peer_id(peer),
                device_id_type=MESH,
            ).start()
            return carry

        lax.fori_loop(1, count, start, 0)
        dst[me] = src[me]

    def exchange_done(src, dst, sem, count, peer_id):
        done = pltpu.make_async_remote_copy(
            src_ref=src.at[pl.ds(0, count - 1)],
            dst_ref=dst.at[pl.ds(0, count - 1)],
            send_sem=sem.at[0],
            recv_sem=sem.at[1],
            device_id=peer_id(0),
            device_id_type=MESH,
        )
        done.wait_recv()
        done.wait_send()

    def by_dp(peer):
        return (peer, e)

    def by_expert(peer):
        return (g, peer)

    exchange(send_a, recv_a, a_sem, ndp, g, by_dp)

    spread_tok = (iota((ndp, ncol), 1) // Q == iota((ndp, ncol), 0)).astype(F32)
    names = mm(ids_ref[...].astype(F32), spread_tok, 0, 0)
    weights = mm(gates_ref[...], spread_tok, 0, 0, HIGH)
    vcol[...] = names
    expert_row = iota((nexp, ncol), 0).astype(F32)
    member = jnp.zeros((nexp, ncol), F32)
    weight = jnp.zeros((nexp, ncol), F32)
    for k in range(top):
        hit = names[k : k + 1, :] == expert_row
        member = jnp.where(hit, 1.0, member)
        weight = jnp.where(hit, weights[k : k + 1, :], weight)
    earlier = jnp.logical_and(
        iota((ncol, ncol), 0) // Q < iota((ncol, ncol), 1) // Q,
        lax.rem(iota((ncol, ncol), 0), Q) == 0,
    )
    rank = mm(member.astype(BF16), earlier.astype(F32).astype(BF16))
    slot_of = jnp.where(member > 0.0, rank, -1.0)
    cube = (nexp, J, ncol)
    slot3 = jnp.broadcast_to(slot_of[:, None, :], cube)
    weight3 = jnp.broadcast_to(weight[:, None, :], cube)
    jrow = iota((J, ncol), 0)
    quarter = lax.rem(iota((J, ncol), 1), Q)
    slot_j = lax.rem(jrow, SLOTS)
    used = jrow < 4 * SLOTS
    first = jrow < 2 * SLOTS
    same = jnp.logical_and(jrow // SLOTS == quarter, used)
    slot_want = jnp.where(same, slot_j, 99).astype(F32)[None]
    placed = slot3 == slot_want
    first3 = jnp.broadcast_to(first.astype(F32)[None], cube) > 0.0
    p_out = jnp.where(placed, jnp.where(first3, 1.0, weight3), 0.0).reshape(nexp * J, ncol)
    p_back = jnp.where(placed, jnp.where(first3, weight3, 1.0), 0.0).reshape(nexp * J, ncol)
    pd_hi[...], pd_lo[...] = split2(p_out)
    pr_hi[...], pr_lo[...] = split2(p_back.T)
    cross = jnp.logical_and(jrow // SLOTS + 2 == quarter, first)
    cross_want = jnp.where(cross, slot_j, 99).astype(F32)[None]
    score_mask[...] = jnp.where(slot3 == cross_want, 1.0, 0.0).reshape(nexp * J, ncol)

    perm_shape = (4 * SLOTS * GROUP, GROUP * J)
    perm_row, perm_col = iota(perm_shape, 0), iota(perm_shape, 1)
    perm = jnp.logical_and(
        perm_row // GROUP == lax.rem(perm_col, J), lax.rem(perm_row, GROUP) == perm_col // J
    )
    perm = perm.astype(F32).astype(BF16)

    exchange_done(send_a, recv_a, a_sem, ndp, by_dp)
    mine = recv_a[...].reshape(ncol, LANES).astype(BF16)
    sent = mm(pd_hi[...], mine) + mm(pd_lo[...], mine)
    send_b[...] = sent.astype(BF16).reshape(nexp, J, LANES)
    exchange(send_b, recv_b, b_sem, nexp, e, by_expert)
    exchange_done(send_b, recv_b, b_sem, nexp, by_expert)

    def place_of(kind, slot, group):
        row = slot * nexp + group * GROUP
        return kind, row // half_rows, row % half_rows

    for group in range(nexp // GROUP):
        block = recv_b[group * GROUP : (group + 1) * GROUP].reshape(GROUP * J, LANES)
        sorted_rows = mm(perm, block).astype(BF16)
        for j in range(4 * SLOTS):
            kind, half, slot = j // (2 * SLOTS), (j // SLOTS) % 2, j % SLOTS
            kind, part_of, row = place_of(kind, slot, group)
            gath[g, kind, part_of, row : row + GROUP, half * LANES : (half + 1) * LANES] = (
                sorted_rows[j * GROUP : (j + 1) * GROUP]
            )

    pieces = [(0, 0), (0, 1), (1, 0), (1, 1)]

    def origin(direction, step, which):
        return at_z(-step if direction == 0 else step, which)

    def goes(direction, step, piece):
        return step < far or (step == far and pieces[piece][1] == direction)

    def ring_copy(direction, step, piece):
        kind, part_of = pieces[piece]
        spot = gath.at[origin(direction, step, core), kind, part_of]
        return pltpu.make_async_remote_copy(
            src_ref=spot,
            dst_ref=spot,
            send_sem=ag_send.at[direction, step, piece],
            recv_sem=ag_recv.at[direction, step, piece],
            device_id=(toward[direction], e),
            device_id_type=MESH,
        )

    def arrival(direction, step, piece):
        kind, part_of = pieces[piece]
        spot = gath.at[origin(direction, step + 1, core), kind, part_of]
        return pltpu.make_async_remote_copy(
            src_ref=spot,
            dst_ref=spot,
            send_sem=ag_send.at[direction, step, piece],
            recv_sem=ag_recv.at[direction, step, piece],
            device_id=(toward[direction], e),
            device_id_type=MESH,
        )

    def sib_copy(direction, step, piece, which):
        kind, part_of = pieces[piece]
        spot = gath.at[origin(direction, step, which), kind, part_of]
        return pltpu.make_async_remote_copy(
            src_ref=spot,
            dst_ref=spot,
            send_sem=sibg_send.at[direction, step, piece],
            recv_sem=sibg_recv.at[direction, step, piece],
            device_id=(sibling, e),
            device_id_type=MESH,
        )

    def own_copy(which):
        spot = gath.at[z * 2 + which]
        return pltpu.make_async_remote_copy(
            src_ref=spot,
            dst_ref=spot,
            send_sem=own_sem.at[0],
            recv_sem=own_sem.at[1],
            device_id=(sibling, e),
            device_id_type=MESH,
        )

    for piece in range(4):
        for direction in range(2):
            if goes(direction, 1, piece):
                ring_copy(direction, 0, piece).start()
    own_copy(core).start()
    for step in range(1, far + 1):
        for piece in range(4):
            for direction in range(2):
                if goes(direction, step, piece):
                    arrival(direction, step - 1, piece).wait_recv()
                    if goes(direction, step + 1, piece):
                        ring_copy(direction, step, piece).start()
                    sib_copy(direction, step, piece, core).start()
    own_copy(other).wait_recv()
    for step in range(1, far + 1):
        for piece in range(4):
            for direction in range(2):
                if goes(direction, step, piece):
                    sib_copy(direction, step, piece, other).wait_recv()

    for load in loads:
        load.wait()

    def held(block, kind):
        return gath[block, kind].reshape(rows, ds)

    def columns(block):
        return pl.ds(pl.multiple_of(block * ds, ds), ds)

    pre = jnp.zeros((rows, 2 * ff), F32)
    back = jnp.zeros((rows, ff), F32)
    for block in range(ndp):
        pre += mm(held(block, 0), wgu[:, block * ds : (block + 1) * ds], 1, 1)
        back += mm(held(block, 1), wd[:, block * ds : (block + 1) * ds], 1, 1)
    gate_pre = pre[:, :ff]
    up_pre = pre[:, ff:]
    logistic = 1.0 / (1.0 + jnp.exp(-gate_pre))
    silu = gate_pre * logistic
    hidden = (silu * up_pre).astype(BF16)
    act_gate = back * up_pre * logistic * (1.0 + gate_pre * (1.0 - logistic))
    act_up = back * silu
    acts = jnp.concatenate([act_gate, act_up], axis=1).astype(BF16)

    def make_part(block):
        out = mm(hidden, wd[:, columns(block)]).astype(BF16)
        part[block, 0] = out.reshape(2, half_rows, ds)
        out = mm(acts, wgu[:, columns(block)]).astype(BF16)
        part[block, 1] = out.reshape(2, half_rows, ds)

    def pair_copy(place, which):
        return pltpu.make_async_remote_copy(
            src_ref=part.at[at_z(place, which)],
            dst_ref=sib_rx.at[at_z(place, 0) // 2],
            send_sem=sibr_send.at[place],
            recv_sem=sibr_recv.at[place],
            device_id=(sibling, e),
            device_id_type=MESH,
        )

    order = [far]
    for away in range(far - 1, 0, -1):
        order += [away, nz - away]
    order += [0]
    for place in order:
        make_part(at_z(place, other))
        pair_copy(place, other).start()
        make_part(at_z(place, core))

    def chain_copy(direction, step, piece):
        return pltpu.make_async_remote_copy(
            src_ref=ring_tx.at[direction, step, piece],
            dst_ref=ring_rx.at[direction, step, piece],
            send_sem=rs_send.at[direction, step, piece],
            recv_sem=rs_recv.at[direction, step, piece],
            device_id=(toward[direction], e),
            device_id_type=MESH,
        )

    def chip_sum(place, piece):
        kind, part_of = pieces[piece]
        return part[at_z(place, core), kind, part_of].astype(F32) + sib_rx[
            at_z(place, 0) // 2, kind, part_of
        ].astype(F32)

    def weight_grads(blocks):
        for block in blocks:
            cols = slice(block * ds, (block + 1) * ds)
            gu_out[:, cols] = mm(acts, held(block, 0), 0, 0).astype(BF16)
            d_out[:, cols] = mm(hidden, held(block, 1), 0, 0).astype(BF16)

    share = -(-ndp // far)
    for step in range(far):
        away = far - step
        places = (away, (nz - away) % nz)
        for place in sorted(set(places)):
            pair_copy(place, other).wait_recv()
        order = [1, 3, 0, 2]
        for turn in range(2):
            for piece in order[2 * turn : 2 * turn + 2] if step else range(2 * turn, 2 * turn + 2):
                for direction in range(2):
                    fresh = pieces[piece][1] != direction
                    if step == 0 and fresh:
                        continue
                    total = chip_sum(places[direction], piece)
                    if step > 1 or (step == 1 and not fresh):
                        chain_copy(direction, step - 1, piece).wait_recv()
                        total += ring_rx[direction, step - 1, piece].astype(F32)
                    ring_tx[direction, step, piece] = total.astype(BF16)
                    chain_copy(direction, step, piece).start()
        weight_grads(range(step * share, min(ndp, (step + 1) * share)))
    stores = [
        pltpu.make_async_copy(gu_out.at[pl.ds(0, ff)], wgg_ref.at[0], o_sem.at[0]),
        pltpu.make_async_copy(gu_out.at[pl.ds(ff, ff)], wug_ref.at[0], o_sem.at[1]),
        pltpu.make_async_copy(d_out, wdg_ref.at[0], o_sem.at[2]),
    ]
    for store in stores:
        store.start()
    pair_copy(0, other).wait_recv()
    final = [None] * 4
    for piece in [1, 3, 0, 2]:
        total = chip_sum(0, piece)
        for direction in range(2):
            if far > 1 or pieces[piece][1] == direction:
                chain_copy(direction, far - 1, piece).wait_recv()
                total += ring_rx[direction, far - 1, piece].astype(F32)
        final[piece] = total.astype(BF16)

    unperm_shape = (GROUP * J, 4 * SLOTS * GROUP)
    un_row, un_col = iota(unperm_shape, 0), iota(unperm_shape, 1)
    unperm = jnp.logical_and(
        un_col // GROUP == lax.rem(un_row, J), lax.rem(un_col, GROUP) == un_row // J
    )
    unperm = unperm.astype(F32).astype(BF16)
    for group in range(nexp // GROUP):
        taken = []
        for j in range(4 * SLOTS):
            kind, half, slot = j // (2 * SLOTS), (j // SLOTS) % 2, j % SLOTS
            kind, part_of, row = place_of(kind, slot, group)
            taken.append(
                final[2 * kind + part_of][row : row + GROUP, half * LANES : (half + 1) * LANES]
            )
        block = mm(unperm, jnp.concatenate(taken, axis=0)).astype(BF16)
        send_c[group * GROUP : (group + 1) * GROUP] = block.reshape(GROUP, J, LANES)
    exchange(send_c, recv_c, c_sem, nexp, e, by_expert)
    exchange_done(send_c, recv_c, c_sem, nexp, by_expert)

    came = recv_c[...].reshape(nexp * J, LANES)
    result = mm(pr_hi[...], came) + mm(pr_lo[...], came)
    products = mm(came, recv_a[...].reshape(ncol, LANES).astype(BF16), 1, 1) * score_mask[...]
    per_expert = jnp.sum(products.reshape(nexp, J, ncol), axis=1)
    names = vcol[...]
    expert_row = iota((nexp, ncol), 0).astype(F32)
    scores = [
        jnp.sum(jnp.where(names[k : k + 1, :] == expert_row, per_expert, 0.0), axis=0, keepdims=True)
        for k in range(top)
    ]
    scores = jnp.concatenate(scores + [jnp.zeros((LANES - top, ncol), F32)], axis=0)
    pick = jnp.logical_and(
        iota((ncol, ncol), 0) // Q == iota((ncol, ncol), 1) // Q,
        lax.rem(iota((ncol, ncol), 0), Q) == 4,
    ).astype(F32)
    result += mm(pick, scores, 1, 1, HIGH)
    send_d[...] = result.reshape(ndp, Q, LANES)
    exchange(send_d, recv_d, d_sem, ndp, g, by_dp)
    exchange_done(send_d, recv_d, d_sem, ndp, by_dp)
    out_cols, grad_cols = [], []
    total = jnp.zeros((1, LANES), F32)
    for came_from in range(ndp):
        for half in range(2):
            out_cols.append(recv_d[came_from, half : half + 1, :])
            grad_cols.append(recv_d[came_from, 2 + half : 3 + half, :])
        total += recv_d[came_from, 4:5, :]
    mixed_ref[...] = jnp.concatenate(out_cols, axis=1).astype(BF16)
    tgrad_ref[...] = jnp.concatenate(grad_cols, axis=1).astype(BF16)
    ggrad_ref[...] = total[:, :top]

    own_copy(core).wait_send()
    for step in range(far + 1):
        for piece in range(4):
            for direction in range(2):
                if step < far and goes(direction, step + 1, piece):
                    ring_copy(direction, step, piece).wait_send()
                if step > 0 and goes(direction, step, piece):
                    sib_copy(direction, step, piece, core).wait_send()
                if step < far and (step > 0 or pieces[piece][1] == direction):
                    chain_copy(direction, step, piece).wait_send()
    for place in range(nz):
        pair_copy(place, other).wait_send()
    for store in stores:
        store.wait()


def on_device(tokens, expert_ids, gates, w_gate, w_up, w_down, cotangent):
    ndp, nexp = lax.axis_size("dp"), lax.axis_size("expert")
    nz, far = ndp // 2, ndp // 4
    ff, width = w_down.shape[1:]
    rows = SLOTS * nexp
    half_rows, ds, ncol = rows // 2, 2 * LANES, ndp * Q
    vmem, hbm = pl.BlockSpec(memory_space=pltpu.VMEM), pl.BlockSpec(memory_space=pl.ANY)
    row = jax.ShapeDtypeStruct(tokens.shape, BF16)
    weight = jax.ShapeDtypeStruct(w_down.shape, BF16)
    dma = pltpu.SemaphoreType.DMA
    return pl.pallas_call(
        functools.partial(kernel, ndp, nexp),
        out_shape=(
            row,
            row,
            jax.ShapeDtypeStruct((1, expert_ids.shape[1]), F32),
            weight,
            weight,
            weight,
        ),
        in_specs=[vmem, vmem, vmem, vmem, hbm, hbm, hbm],
        out_specs=(vmem, vmem, vmem, hbm, hbm, hbm),
        scratch_shapes=[
            pltpu.VMEM((2 * ff, width), BF16),
            pltpu.VMEM((ff, width), BF16),
            pltpu.VMEM((2 * ff, width), BF16),
            pltpu.VMEM((ff, width), BF16),
            pltpu.VMEM((ndp, Q, LANES), F32),
            pltpu.VMEM((ndp, Q, LANES), F32),
            pltpu.VMEM((nexp, J, LANES), BF16),
            pltpu.VMEM((nexp, J, LANES), BF16),
            pltpu.VMEM((ndp, 2, 2, half_rows, ds), BF16),
            pltpu.VMEM((ndp, 2, 2, half_rows, ds), BF16),
            pltpu.VMEM((nz, 2, 2, half_rows, ds), BF16),
            pltpu.VMEM((2, far, 4, half_rows, ds), BF16),
            pltpu.VMEM((2, far, 4, half_rows, ds), BF16),
            pltpu.VMEM((nexp, J, LANES), BF16),
            pltpu.VMEM((nexp, J, LANES), BF16),
            pltpu.VMEM((ndp, Q, LANES), F32),
            pltpu.VMEM((ndp, Q, LANES), F32),
            pltpu.VMEM((nexp * J, ncol), BF16),
            pltpu.VMEM((nexp * J, ncol), BF16),
            pltpu.VMEM((ncol, nexp * J), BF16),
            pltpu.VMEM((ncol, nexp * J), BF16),
            pltpu.VMEM((nexp * J, ncol), F32),
            pltpu.VMEM((expert_ids.shape[1], ncol), F32),
            dma((3,)),
            dma((3,)),
            dma((2,)),
            dma((2,)),
            dma((2,)),
            dma((2,)),
            dma((2, far, 4)),
            dma((2, far, 4)),
            dma((2, far + 1, 4)),
            dma((2, far + 1, 4)),
            dma((2,)),
            dma((nz,)),
            dma((nz,)),
            dma((2, far, 4)),
            dma((2, far, 4)),
        ],
        compiler_params=pltpu.CompilerParams(
            collective_id=0, has_side_effects=True, vmem_limit_bytes=48 * 1024 * 1024
        ),
        cost_estimate=pl.CostEstimate(
            flops=18 * rows * ff * width, bytes_accessed=6 * ff * width * 2, transcendentals=rows * ff
        ),
    )(tokens, cotangent, expert_ids, gates, w_gate, w_up, w_down)


def solution(mesh):
    placed = (
        P(("expert", "dp"), None),
        P("expert", None),
        P("expert", None),
        P("expert", "dp", None),
        P("expert", "dp", None),
        P("expert", "dp", None),
        P(("expert", "dp"), None),
    )
    return jax.shard_map(
        on_device,
        mesh=mesh,
        in_specs=placed,
        out_specs=(
            P(("expert", "dp"), None),
            P(("expert", "dp"), None),
            P(("expert", "dp"), None),
            P("expert", "dp", None),
            P("expert", "dp", None),
            P("expert", "dp", None),
        ),
        check_vma=False,
    )
```

```python
import functools

import jax
import jax.numpy as jnp
from jax import lax
from jax.experimental import pallas as pl
from jax.experimental.pallas import tpu as pltpu
from jax.sharding import PartitionSpec as P

F32 = jnp.float32
BF16 = jnp.bfloat16
MESH = pl.DeviceIdType.MESH
SLOTS = 3
LANES = 128
Q = 8
J = 16
GROUP = 16
HIGH = lax.Precision.HIGHEST


def mm(left, right, left_dim=1, right_dim=0, precision=None):
    return lax.dot_general(
        left,
        right,
        (((left_dim,), (right_dim,)), ((), ())),
        preferred_element_type=F32,
        precision=precision,
    )


def iota(shape, dim):
    return lax.broadcasted_iota(jnp.int32, shape, dim)


def split2(value):
    high = value.astype(BF16)
    return high, (value - high.astype(F32)).astype(BF16)


def kernel(
    ndp,
    nexp,
    tok_hbm,
    cot_hbm,
    ids_hbm,
    gates_hbm,
    wg_ref,
    wu_ref,
    wd_ref,
    mixed_ref,
    tgrad_ref,
    ggrad_ref,
    wgg_ref,
    wug_ref,
    wdg_ref,
    tok_ref,
    cot_ref,
    ids_ref,
    gates_ref,
    wgu,
    wd,
    gu_out,
    d_out,
    send_a,
    recv_a,
    send_b,
    recv_b,
    gath,
    part,
    sib_rx,
    ring_tx,
    ring_rx,
    send_c,
    recv_c,
    send_d,
    recv_d,
    pd_hi,
    pd_lo,
    pr_hi,
    pr_lo,
    score_mask,
    vcol,
    slots_kept,
    weight_kept,
    i_sem,
    w_sem,
    o_sem,
    a_sem,
    b_sem,
    c_sem,
    d_sem,
    ag_send,
    ag_recv,
    sibg_send,
    sibg_recv,
    sibr_send,
    sibr_recv,
    rs_send,
    rs_recv,
):
    g = lax.axis_index("dp")
    e = lax.axis_index("expert")
    nz = ndp // 2
    far = nz // 2
    z = g // 2
    core = lax.rem(g, 2)
    other = 1 - core
    rows = SLOTS * nexp
    half_rows = rows // 2
    hexp = nexp // 2
    ff = wd.shape[0]
    ncol = ndp * Q
    ds = 2 * LANES
    top = ids_ref.shape[0]

    def at_z(offset, which):
        return lax.rem(z + offset + nz, nz) * 2 + which

    right = at_z(1, core)
    left = at_z(-1, core)
    sibling = z * 2 + other
    toward = (right, left)

    small = [
        pltpu.make_async_copy(tok_hbm, tok_ref, i_sem.at[0]),
        pltpu.make_async_copy(cot_hbm, cot_ref, i_sem.at[1]),
        pltpu.make_async_copy(ids_hbm, ids_ref, i_sem.at[2]),
        pltpu.make_async_copy(gates_hbm, gates_ref, i_sem.at[3]),
    ]
    for load in small:
        load.start()

    barrier = pltpu.get_barrier_semaphore()

    def greet_dp(i, carry):
        pl.semaphore_signal(
            barrier, inc=1, device_id=(lax.rem(g + i, ndp), e), device_id_type=MESH
        )
        return carry

    def greet_expert(i, carry):
        pl.semaphore_signal(
            barrier, inc=1, device_id=(g, lax.rem(e + i, nexp)), device_id_type=MESH
        )
        return carry

    lax.fori_loop(1, ndp, greet_dp, 0)
    lax.fori_loop(1, nexp, greet_expert, 0)

    loads = [
        pltpu.make_async_copy(wg_ref.at[0], wgu.at[pl.ds(0, ff)], w_sem.at[0]),
        pltpu.make_async_copy(wu_ref.at[0], wgu.at[pl.ds(ff, ff)], w_sem.at[1]),
        pltpu.make_async_copy(wd_ref.at[0], wd, w_sem.at[2]),
    ]
    for load in loads:
        load.start()

    for load in small:
        load.wait()
    token = tok_ref[...].astype(F32)
    cotan = cot_ref[...].astype(F32)
    send_a[...] = jnp.zeros(send_a.shape, F32)
    for to in range(ndp):
        for half in range(2):
            lane = to * ds + half * LANES
            send_a[to, half : half + 1, :] = token[:, lane : lane + LANES]
            send_a[to, 2 + half : 3 + half, :] = cotan[:, lane : lane + LANES]

    pl.semaphore_wait(barrier, ndp - 1 + nexp - 1)

    def exchange(src, dst, sem, count, me, peer_id):
        def start(i, carry):
            peer = lax.rem(me + i, count)
            pltpu.make_async_remote_copy(
                src_ref=src.at[peer],
                dst_ref=dst.at[me],
                send_sem=sem.at[0],
                recv_sem=sem.at[1],
                device_id=peer_id(peer),
                device_id_type=MESH,
            ).start()
            return carry

        lax.fori_loop(1, count, start, 0)
        dst[me] = src[me]

    def exchange_done(src, dst, sem, count, peer_id):
        done = pltpu.make_async_remote_copy(
            src_ref=src.at[pl.ds(0, count - 1)],
            dst_ref=dst.at[pl.ds(0, count - 1)],
            send_sem=sem.at[0],
            recv_sem=sem.at[1],
            device_id=peer_id(0),
            device_id_type=MESH,
        )
        done.wait_recv()
        done.wait_send()

    def by_dp(peer):
        return (peer, e)

    def expert_start(src, dst, sem, span, way):
        def start(i, carry):
            pltpu.make_async_remote_copy(
                src_ref=src.at[i],
                dst_ref=dst.at[i],
                send_sem=sem.at[2 * span],
                recv_sem=sem.at[2 * span + 1],
                device_id=(g, lax.rem(e + way * i + nexp, nexp)),
                device_id_type=MESH,
            ).start()
            return carry

        lax.fori_loop(max(1, span * hexp), (span + 1) * hexp, start, 0)
        if span == 0:
            dst[0] = src[0]

    def expert_round(src, dst, sem, span):
        blocks = pl.ds(max(1, span * hexp), (span + 1) * hexp - max(1, span * hexp))
        return pltpu.make_async_remote_copy(
            src_ref=src.at[blocks],
            dst_ref=dst.at[blocks],
            send_sem=sem.at[2 * span],
            recv_sem=sem.at[2 * span + 1],
            device_id=(g, e),
            device_id_type=MESH,
        )

    exchange(send_a, recv_a, a_sem, ndp, g, by_dp)

    spread_tok = (iota((ndp, ncol), 1) // Q == iota((ndp, ncol), 0)).astype(F32)
    names = mm(ids_ref[...].astype(F32), spread_tok)
    weights = mm(gates_ref[...], spread_tok, precision=HIGH)
    vcol[...] = names
    expert_row = lax.rem(iota((nexp, ncol), 0) + e, nexp).astype(F32)
    member = jnp.zeros((nexp, ncol), F32)
    weight = jnp.zeros((nexp, ncol), F32)
    for k in range(top):
        hit = names[k : k + 1, :] == expert_row
        member = jnp.where(hit, 1.0, member)
        weight = jnp.where(hit, weights[k : k + 1, :], weight)
    earlier = jnp.logical_and(
        iota((ncol, ncol), 0) // Q < iota((ncol, ncol), 1) // Q,
        lax.rem(iota((ncol, ncol), 0), Q) == 0,
    )
    rank = mm(member.astype(BF16), earlier.astype(F32).astype(BF16))
    slot_of = jnp.where(member > 0.0, rank, -1.0)
    cube = (nexp, J, ncol)
    slot3 = jnp.broadcast_to(slot_of[:, None, :], cube)
    weight3 = jnp.broadcast_to(weight[:, None, :], cube)
    jrow = iota((J, ncol), 0)
    quarter = lax.rem(iota((J, ncol), 1), Q)
    slot_j = lax.rem(jrow, SLOTS)
    used = jrow < 4 * SLOTS
    first = jrow < 2 * SLOTS
    same = jnp.logical_and(jrow // SLOTS == quarter, used)
    slot_want = jnp.where(same, slot_j, 99).astype(F32)[None]
    placed = slot3 == slot_want
    first3 = jnp.broadcast_to(first.astype(F32)[None], cube) > 0.0
    p_out = jnp.where(placed, jnp.where(first3, 1.0, weight3), 0.0).reshape(nexp * J, ncol)
    pd_hi[...], pd_lo[...] = split2(p_out)
    slots_kept[...] = slot_of
    weight_kept[...] = weight

    perm_shape = (4 * SLOTS * GROUP, GROUP * J)
    perm_row, perm_col = iota(perm_shape, 0), iota(perm_shape, 1)
    perm = jnp.logical_and(
        perm_row // GROUP == lax.rem(perm_col, J), lax.rem(perm_row, GROUP) == perm_col // J
    )
    perm = perm.astype(F32).astype(BF16)

    exchange_done(send_a, recv_a, a_sem, ndp, by_dp)
    mine = recv_a[...].reshape(ncol, LANES).astype(BF16)
    half_block = hexp * J
    for span in range(2):
        lines = slice(span * half_block, (span + 1) * half_block)
        sent = mm(pd_hi[lines], mine) + mm(pd_lo[lines], mine)
        send_b[span * hexp : (span + 1) * hexp] = sent.astype(BF16).reshape(hexp, J, LANES)
        expert_start(send_b, recv_b, b_sem, span, 1)

    def place_of(slot, group):
        per_half = hexp // GROUP
        return group // per_half, slot * hexp + group % per_half * GROUP

    def groups_of(span):
        return range(span * hexp // GROUP, (span + 1) * hexp // GROUP)

    def unpack(span):
        for group in groups_of(span):
            block = recv_b[group * GROUP : (group + 1) * GROUP].reshape(GROUP * J, LANES)
            sorted_rows = mm(perm, block).astype(BF16)
            for j in range(4 * SLOTS):
                kind, half, slot = j // (2 * SLOTS), (j // SLOTS) % 2, j % SLOTS
                part_of, row = place_of(slot, group)
                gath[
                    g, kind, part_of, row : row + GROUP, half * LANES : (half + 1) * LANES
                ] = sorted_rows[j * GROUP : (j + 1) * GROUP]

    pieces = [(0, 0), (1, 0), (0, 1), (1, 1)]

    def origin(direction, step, which):
        return at_z(-step if direction == 0 else step, which)

    def goes(direction, step, piece):
        return step < far or (step == far and pieces[piece][1] == direction)

    def ring_copy(direction, step, piece):
        kind, part_of = pieces[piece]
        spot = gath.at[origin(direction, step, core), kind, part_of]
        return pltpu.make_async_remote_copy(
            src_ref=spot,
            dst_ref=spot,
            send_sem=ag_send.at[direction, step, piece],
            recv_sem=ag_recv.at[direction, step, piece],
            device_id=(toward[direction], e),
            device_id_type=MESH,
        )

    def arrival(direction, step, piece):
        kind, part_of = pieces[piece]
        spot = gath.at[origin(direction, step + 1, core), kind, part_of]
        return pltpu.make_async_remote_copy(
            src_ref=spot,
            dst_ref=spot,
            send_sem=ag_send.at[direction, step, piece],
            recv_sem=ag_recv.at[direction, step, piece],
            device_id=(toward[direction], e),
            device_id_type=MESH,
        )

    def sib_copy(direction, step, piece, which):
        kind, part_of = pieces[piece]
        spot = gath.at[origin(direction, step, which), kind, part_of]
        return pltpu.make_async_remote_copy(
            src_ref=spot,
            dst_ref=spot,
            send_sem=sibg_send.at[direction, step, piece],
            recv_sem=sibg_recv.at[direction, step, piece],
            device_id=(sibling, e),
            device_id_type=MESH,
        )

    for span in range(2):
        expert_round(send_b, recv_b, b_sem, span).wait_recv()
        unpack(span)
        for piece in (2 * span, 2 * span + 1):
            for direction in range(2):
                if goes(direction, 1, piece):
                    ring_copy(direction, 0, piece).start()
            sib_copy(0, 0, piece, core).start()

    slot3 = jnp.broadcast_to(slots_kept[...][:, None, :], cube)
    weight3 = jnp.broadcast_to(weight_kept[...][:, None, :], cube)
    placed = slot3 == slot_want
    p_back = jnp.where(placed, jnp.where(first3, weight3, 1.0), 0.0).reshape(nexp * J, ncol)
    pr_hi[...], pr_lo[...] = split2(p_back.T)
    cross = jnp.logical_and(jrow // SLOTS + 2 == quarter, first)
    cross_want = jnp.where(cross, slot_j, 99).astype(F32)[None]
    score_mask[...] = jnp.where(slot3 == cross_want, 1.0, 0.0).reshape(nexp * J, ncol)

    for step in range(1, far + 1):
        for piece in range(4):
            for direction in range(2):
                if goes(direction, step, piece):
                    arrival(direction, step - 1, piece).wait_recv()
                    if goes(direction, step + 1, piece):
                        ring_copy(direction, step, piece).start()
                    sib_copy(direction, step, piece, core).start()
    for piece in range(4):
        sib_copy(0, 0, piece, other).wait_recv()
    for step in range(1, far + 1):
        for piece in range(4):
            for direction in range(2):
                if goes(direction, step, piece):
                    sib_copy(direction, step, piece, other).wait_recv()

    for load in loads:
        load.wait()

    def held(block, kind):
        return gath[block, kind].reshape(rows, ds)

    def columns(block):
        return pl.ds(pl.multiple_of(block * ds, ds), ds)

    pre = jnp.zeros((rows, 2 * ff), F32)
    back = jnp.zeros((rows, ff), F32)
    for block in range(ndp):
        pre += mm(held(block, 0), wgu[:, block * ds : (block + 1) * ds], 1, 1)
        back += mm(held(block, 1), wd[:, block * ds : (block + 1) * ds], 1, 1)
    gate_pre = pre[:, :ff]
    up_pre = pre[:, ff:]
    logistic = 1.0 / (1.0 + jnp.exp(-gate_pre))
    silu = gate_pre * logistic
    hidden = (silu * up_pre).astype(BF16)
    act_gate = back * up_pre * logistic * (1.0 + gate_pre * (1.0 - logistic))
    act_up = back * silu
    acts = jnp.concatenate([act_gate, act_up], axis=1).astype(BF16)

    def make_part(block):
        out = mm(hidden, wd[:, columns(block)]).astype(BF16)
        part[block, 0] = out.reshape(2, half_rows, ds)
        out = mm(acts, wgu[:, columns(block)]).astype(BF16)
        part[block, 1] = out.reshape(2, half_rows, ds)

    def pair_copy(place, which):
        return pltpu.make_async_remote_copy(
            src_ref=part.at[at_z(place, which)],
            dst_ref=sib_rx.at[at_z(place, 0) // 2],
            send_sem=sibr_send.at[place],
            recv_sem=sibr_recv.at[place],
            device_id=(sibling, e),
            device_id_type=MESH,
        )

    def make_parts(places):
        for place in places:
            make_part(at_z(place, other))
            pair_copy(place, other).start()
            make_part(at_z(place, core))

    def at_distance(away):
        return sorted({away, (nz - away) % nz})

    make_parts(at_distance(far))
    make_parts(at_distance(far - 1))

    def chain_copy(direction, step, piece):
        return pltpu.make_async_remote_copy(
            src_ref=ring_tx.at[direction, step, piece],
            dst_ref=ring_rx.at[direction, step, piece],
            send_sem=rs_send.at[direction, step, piece],
            recv_sem=rs_recv.at[direction, step, piece],
            device_id=(toward[direction], e),
            device_id_type=MESH,
        )

    def chip_sum(place, piece):
        kind, part_of = pieces[piece]
        return part[at_z(place, core), kind, part_of].astype(F32) + sib_rx[
            at_z(place, 0) // 2, kind, part_of
        ].astype(F32)

    def weight_grads(blocks):
        for block in blocks:
            cols = slice(block * ds, (block + 1) * ds)
            gu_out[:, cols] = mm(acts, held(block, 0), 0, 0).astype(BF16)
            d_out[:, cols] = mm(hidden, held(block, 1), 0, 0).astype(BF16)

    if far == 4:
        turns = (
            [(0, 0), (0, 1), (1, 2), (1, 3), (1, 0), (1, 1), (2, 2), (2, 0), (2, 1), (2, 3)]
            + [(3, 0), (3, 1), (3, 2), (3, 3)],
            [(0, 2), (0, 3)] + [(step, piece) for step in range(1, far) for piece in range(4)],
        )
    else:
        turns = tuple(
            [(0, 2 * way), (0, 2 * way + 1)]
            + [
                (step, piece)
                for step in range(1, far)
                for piece in ((2, 3, 0, 1), (0, 1, 2, 3))[way]
            ]
            for way in range(2)
        )
    count = len(turns[0])
    paired = set()
    made = far - 1
    done_blocks = 0
    for turn in range(count):
        for direction in range(2):
            step, piece = turns[direction][turn]
            away = far - step
            place = away if direction == 0 else (nz - away) % nz
            if place not in paired:
                pair_copy(place, other).wait_recv()
                paired.add(place)
            total = chip_sum(place, piece)
            if step > (0 if pieces[piece][1] == direction else 1):
                chain_copy(direction, step - 1, piece).wait_recv()
                total += ring_rx[direction, step - 1, piece].astype(F32)
            ring_tx[direction, step, piece] = total.astype(BF16)
            chain_copy(direction, step, piece).start()
        if turn % 3 == 2 and made > 0:
            made -= 1
            make_parts(at_distance(made))
        elif turn > 2:
            weight_grads(range(done_blocks, min(ndp, done_blocks + 2)))
            done_blocks = min(ndp, done_blocks + 2)
    weight_grads(range(done_blocks, ndp))
    stores = [
        pltpu.make_async_copy(gu_out.at[pl.ds(0, ff)], wgg_ref.at[0], o_sem.at[0]),
        pltpu.make_async_copy(gu_out.at[pl.ds(ff, ff)], wug_ref.at[0], o_sem.at[1]),
        pltpu.make_async_copy(d_out, wdg_ref.at[0], o_sem.at[2]),
    ]
    for store in stores:
        store.start()
    pair_copy(0, other).wait_recv()
    unperm_shape = (GROUP * J, 4 * SLOTS * GROUP)
    un_row, un_col = iota(unperm_shape, 0), iota(unperm_shape, 1)
    unperm = jnp.logical_and(
        un_col // GROUP == lax.rem(un_row, J), lax.rem(un_col, GROUP) == un_row // J
    )
    unperm = unperm.astype(F32).astype(BF16)
    for span in range(2):
        final = []
        for piece in (2 * span, 2 * span + 1):
            total = chip_sum(0, piece)
            for direction in range(2):
                if far > 1 or pieces[piece][1] == direction:
                    chain_copy(direction, far - 1, piece).wait_recv()
                    total += ring_rx[direction, far - 1, piece].astype(F32)
            final.append(total.astype(BF16))
        for group in groups_of(span):
            taken = []
            for j in range(4 * SLOTS):
                kind, half, slot = j // (2 * SLOTS), (j // SLOTS) % 2, j % SLOTS
                row = place_of(slot, group)[1]
                taken.append(
                    final[kind][row : row + GROUP, half * LANES : (half + 1) * LANES]
                )
            block = mm(unperm, jnp.concatenate(taken, axis=0)).astype(BF16)
            send_c[group * GROUP : (group + 1) * GROUP] = block.reshape(GROUP, J, LANES)
        expert_start(send_c, recv_c, c_sem, span, -1)

    result = jnp.zeros((ncol, LANES), F32)
    mine = recv_a[...].reshape(ncol, LANES).astype(BF16)
    by_half = []
    for span in range(2):
        expert_round(send_c, recv_c, c_sem, span).wait_recv()
        came = recv_c[span * hexp : (span + 1) * hexp].reshape(half_block, LANES)
        lines = slice(span * half_block, (span + 1) * half_block)
        result += mm(pr_hi[:, lines], came) + mm(pr_lo[:, lines], came)
        products = mm(came, mine, 1, 1) * score_mask[lines]
        by_half.append(jnp.sum(products.reshape(hexp, J, ncol), axis=1))
    per_expert = jnp.concatenate(by_half, axis=0)
    names = vcol[...]
    expert_row = lax.rem(iota((nexp, ncol), 0) + e, nexp).astype(F32)
    scores = [
        jnp.sum(jnp.where(names[k : k + 1, :] == expert_row, per_expert, 0.0), axis=0, keepdims=True)
        for k in range(top)
    ]
    scores = jnp.concatenate(scores + [jnp.zeros((LANES - top, ncol), F32)], axis=0)
    pick = jnp.logical_and(
        iota((ncol, ncol), 0) // Q == iota((ncol, ncol), 1) // Q,
        lax.rem(iota((ncol, ncol), 0), Q) == 4,
    ).astype(F32)
    result += mm(pick, scores, 1, 1, HIGH)
    send_d[...] = result.reshape(ndp, Q, LANES)
    exchange(send_d, recv_d, d_sem, ndp, g, by_dp)
    exchange_done(send_d, recv_d, d_sem, ndp, by_dp)
    out_cols, grad_cols = [], []
    total = jnp.zeros((1, LANES), F32)
    for came_from in range(ndp):
        for half in range(2):
            out_cols.append(recv_d[came_from, half : half + 1, :])
            grad_cols.append(recv_d[came_from, 2 + half : 3 + half, :])
        total += recv_d[came_from, 4:5, :]
    mixed_ref[...] = jnp.concatenate(out_cols, axis=1).astype(BF16)
    tgrad_ref[...] = jnp.concatenate(grad_cols, axis=1).astype(BF16)
    ggrad_ref[...] = total[:, :top]

    for span in range(2):
        expert_round(send_b, recv_b, b_sem, span).wait_send()
        expert_round(send_c, recv_c, c_sem, span).wait_send()
    for piece in range(4):
        sib_copy(0, 0, piece, core).wait_send()
    for step in range(far + 1):
        for piece in range(4):
            for direction in range(2):
                if step < far and goes(direction, step + 1, piece):
                    ring_copy(direction, step, piece).wait_send()
                if step > 0 and goes(direction, step, piece):
                    sib_copy(direction, step, piece, core).wait_send()
                if step < far and (step > 0 or pieces[piece][1] == direction):
                    chain_copy(direction, step, piece).wait_send()
    for place in range(nz):
        pair_copy(place, other).wait_send()
    for store in stores:
        store.wait()


def on_device(tokens, expert_ids, gates, w_gate, w_up, w_down, cotangent):
    ndp, nexp = lax.axis_size("dp"), lax.axis_size("expert")
    nz, far = ndp // 2, ndp // 4
    ff, width = w_down.shape[1:]
    rows = SLOTS * nexp
    half_rows, ds, ncol = rows // 2, 2 * LANES, ndp * Q
    vmem, hbm = pl.BlockSpec(memory_space=pltpu.VMEM), pl.BlockSpec(memory_space=pl.ANY)
    row = jax.ShapeDtypeStruct(tokens.shape, BF16)
    weight = jax.ShapeDtypeStruct(w_down.shape, BF16)
    dma = pltpu.SemaphoreType.DMA
    outs = pl.pallas_call(
        functools.partial(kernel, ndp, nexp),
        out_shape=(
            row,
            row,
            jax.ShapeDtypeStruct((1, expert_ids.shape[1]), F32),
            weight,
            weight,
            weight,
        ),
        in_specs=[pl.BlockSpec(memory_space=pltpu.HBM)] * 7,
        out_specs=(vmem, vmem, vmem, hbm, hbm, hbm),
        scratch_shapes=[
            pltpu.VMEM(tokens.shape, BF16),
            pltpu.VMEM(tokens.shape, BF16),
            pltpu.VMEM(expert_ids.shape[::-1], jnp.int32),
            pltpu.VMEM(expert_ids.shape[::-1], F32),
            pltpu.VMEM((2 * ff, width), BF16),
            pltpu.VMEM((ff, width), BF16),
            pltpu.VMEM((2 * ff, width), BF16),
            pltpu.VMEM((ff, width), BF16),
            pltpu.VMEM((ndp, Q, LANES), F32),
            pltpu.VMEM((ndp, Q, LANES), F32),
            pltpu.VMEM((nexp, J, LANES), BF16),
            pltpu.VMEM((nexp, J, LANES), BF16),
            pltpu.VMEM((ndp, 2, 2, half_rows, ds), BF16),
            pltpu.VMEM((ndp, 2, 2, half_rows, ds), BF16),
            pltpu.VMEM((nz, 2, 2, half_rows, ds), BF16),
            pltpu.VMEM((2, far, 4, half_rows, ds), BF16),
            pltpu.VMEM((2, far, 4, half_rows, ds), BF16),
            pltpu.VMEM((nexp, J, LANES), BF16),
            pltpu.VMEM((nexp, J, LANES), BF16),
            pltpu.VMEM((ndp, Q, LANES), F32),
            pltpu.VMEM((ndp, Q, LANES), F32),
            pltpu.VMEM((nexp * J, ncol), BF16),
            pltpu.VMEM((nexp * J, ncol), BF16),
            pltpu.VMEM((ncol, nexp * J), BF16),
            pltpu.VMEM((ncol, nexp * J), BF16),
            pltpu.VMEM((nexp * J, ncol), F32),
            pltpu.VMEM((expert_ids.shape[1], ncol), F32),
            pltpu.VMEM((nexp, ncol), F32),
            pltpu.VMEM((nexp, ncol), F32),
            dma((4,)),
            dma((3,)),
            dma((3,)),
            dma((2,)),
            dma((4,)),
            dma((4,)),
            dma((2,)),
            dma((2, far, 4)),
            dma((2, far, 4)),
            dma((2, far + 1, 4)),
            dma((2, far + 1, 4)),
            dma((nz,)),
            dma((nz,)),
            dma((2, far, 4)),
            dma((2, far, 4)),
        ],
        compiler_params=pltpu.CompilerParams(
            collective_id=0, has_side_effects=True, vmem_limit_bytes=61 * 1024 * 1024
        ),
        cost_estimate=pl.CostEstimate(
            flops=18 * rows * ff * width, bytes_accessed=6 * ff * width * 2, transcendentals=rows * ff
        ),
    )(tokens, cotangent, expert_ids.T, gates.T, w_gate, w_up, w_down)
    return pl.pallas_call(
        copy_out,
        out_shape=[jax.ShapeDtypeStruct(out.shape, out.dtype) for out in outs],
        in_specs=[pl.BlockSpec(memory_space=pltpu.HBM)] * 6,
        out_specs=[pl.BlockSpec(memory_space=pltpu.HBM)] * 6,
        scratch_shapes=[pltpu.VMEM(out.shape, out.dtype) for out in outs] + [dma((6,)), dma((6,))],
        compiler_params=pltpu.CompilerParams(vmem_limit_bytes=61 * 1024 * 1024),
    )(*outs)


def copy_out(*refs):
    count = len(refs) // 3
    sources, targets, held = refs[:count], refs[count : 2 * count], refs[2 * count : 3 * count]
    in_sem, out_sem = refs[3 * count :]
    order = range(count)[::-1]
    gets = [pltpu.make_async_copy(sources[i], held[i], in_sem.at[i]) for i in range(count)]
    puts = [pltpu.make_async_copy(held[i], targets[i], out_sem.at[i]) for i in range(count)]
    for i in order:
        gets[i].start()
    for i in order:
        gets[i].wait()
        puts[i].start()
    for i in order:
        puts[i].wait()


def solution(mesh):
    placed = (
        P(("expert", "dp"), None),
        P("expert", None),
        P("expert", None),
        P("expert", "dp", None),
        P("expert", "dp", None),
        P("expert", "dp", None),
        P(("expert", "dp"), None),
    )
    return jax.shard_map(
        on_device,
        mesh=mesh,
        in_specs=placed,
        out_specs=(
            P(("expert", "dp"), None),
            P(("expert", "dp"), None),
            P(("expert", "dp"), None),
            P("expert", "dp", None),
            P("expert", "dp", None),
            P("expert", "dp", None),
        ),
        check_vma=False,
    )
```

```python
import functools

import jax
import jax.numpy as jnp
from jax import lax
from jax.experimental import pallas as pl
from jax.experimental.pallas import tpu as pltpu
from jax.sharding import PartitionSpec as P

F32 = jnp.float32
BF16 = jnp.bfloat16
MESH = pl.DeviceIdType.MESH
SLOTS = 3
LANES = 128
Q = 8
J = 16
GROUP = 16
CHUNKS = 4
HIGH = lax.Precision.HIGHEST


def mm(left, right, left_dim=1, right_dim=0, precision=None):
    return lax.dot_general(
        left,
        right,
        (((left_dim,), (right_dim,)), ((), ())),
        preferred_element_type=F32,
        precision=precision,
    )


def iota(shape, dim):
    return lax.broadcasted_iota(jnp.int32, shape, dim)


def split2(value):
    high = value.astype(BF16)
    return high, (value - high.astype(F32)).astype(BF16)


def kernel(
    ndp,
    nexp,
    tok_hbm,
    cot_hbm,
    ids_hbm,
    gates_hbm,
    wg_ref,
    wu_ref,
    wd_ref,
    mixed_ref,
    tgrad_ref,
    ggrad_ref,
    wgg_ref,
    wug_ref,
    wdg_ref,
    tok_ref,
    cot_ref,
    ids_ref,
    gates_ref,
    wgu,
    wd,
    gu_out,
    d_out,
    send_a,
    recv_a,
    send_b,
    recv_b,
    gath,
    part,
    sib_rx,
    ring_tx,
    ring_rx,
    send_c,
    recv_c,
    send_d,
    recv_d,
    pd_hi,
    pd_lo,
    pr_hi,
    pr_lo,
    score_mask,
    vcol,
    slots_kept,
    weight_kept,
    i_sem,
    w_sem,
    o_sem,
    a_sem,
    b_sem,
    c_sem,
    d_sem,
    ag_send,
    ag_recv,
    sibg_send,
    sibg_recv,
    sibr_send,
    sibr_recv,
    rs_send,
    rs_recv,
):
    g = lax.axis_index("dp")
    e = lax.axis_index("expert")
    nz = ndp // 2
    far = nz // 2
    z = g // 2
    core = lax.rem(g, 2)
    other = 1 - core
    rows = SLOTS * nexp
    cut = SLOTS * GROUP
    parts = nexp // GROUP
    ff = wd.shape[0]
    ncol = ndp * Q
    ds = 2 * LANES
    top = ids_ref.shape[0]

    def at_z(offset, which):
        return lax.rem(z + offset + nz, nz) * 2 + which

    right = at_z(1, core)
    left = at_z(-1, core)
    sibling = z * 2 + other
    toward = (right, left)

    small = [
        pltpu.make_async_copy(tok_hbm, tok_ref, i_sem.at[0]),
        pltpu.make_async_copy(cot_hbm, cot_ref, i_sem.at[1]),
        pltpu.make_async_copy(ids_hbm, ids_ref, i_sem.at[2]),
        pltpu.make_async_copy(gates_hbm, gates_ref, i_sem.at[3]),
    ]
    for load in small:
        load.start()

    barrier = pltpu.get_barrier_semaphore()

    def greet_dp(i, carry):
        pl.semaphore_signal(
            barrier, inc=1, device_id=(lax.rem(g + i, ndp), e), device_id_type=MESH
        )
        return carry

    def greet_expert(i, carry):
        pl.semaphore_signal(
            barrier, inc=1, device_id=(g, lax.rem(e + i, nexp)), device_id_type=MESH
        )
        return carry

    lax.fori_loop(1, ndp, greet_dp, 0)
    lax.fori_loop(1, nexp, greet_expert, 0)

    loads = [
        pltpu.make_async_copy(wg_ref.at[0], wgu.at[pl.ds(0, ff)], w_sem.at[0]),
        pltpu.make_async_copy(wu_ref.at[0], wgu.at[pl.ds(ff, ff)], w_sem.at[1]),
        pltpu.make_async_copy(wd_ref.at[0], wd, w_sem.at[2]),
    ]
    for load in loads:
        load.start()

    for load in small:
        load.wait()
    token = tok_ref[...].astype(F32)
    cotan = cot_ref[...].astype(F32)
    send_a[...] = jnp.zeros(send_a.shape, F32)
    for to in range(ndp):
        for half in range(2):
            lane = to * ds + half * LANES
            send_a[to, half : half + 1, :] = token[:, lane : lane + LANES]
            send_a[to, 2 + half : 3 + half, :] = cotan[:, lane : lane + LANES]

    pl.semaphore_wait(barrier, ndp - 1 + nexp - 1)

    def exchange(src, dst, sem, count, me, peer_id):
        def start(i, carry):
            peer = lax.rem(me + i, count)
            pltpu.make_async_remote_copy(
                src_ref=src.at[peer],
                dst_ref=dst.at[me],
                send_sem=sem.at[0],
                recv_sem=sem.at[1],
                device_id=peer_id(peer),
                device_id_type=MESH,
            ).start()
            return carry

        lax.fori_loop(1, count, start, 0)
        dst[me] = src[me]

    def exchange_done(src, dst, sem, count, peer_id):
        done = pltpu.make_async_remote_copy(
            src_ref=src.at[pl.ds(0, count - 1)],
            dst_ref=dst.at[pl.ds(0, count - 1)],
            send_sem=sem.at[0],
            recv_sem=sem.at[1],
            device_id=peer_id(0),
            device_id_type=MESH,
        )
        done.wait_recv()
        done.wait_send()

    def by_dp(peer):
        return (peer, e)

    def expert_start(src, dst, sem, span, way):
        def start(i, carry):
            pltpu.make_async_remote_copy(
                src_ref=src.at[i],
                dst_ref=dst.at[i],
                send_sem=sem.at[2 * span],
                recv_sem=sem.at[2 * span + 1],
                device_id=(g, lax.rem(e + way * i + nexp, nexp)),
                device_id_type=MESH,
            ).start()
            return carry

        lax.fori_loop(max(1, span * GROUP), (span + 1) * GROUP, start, 0)
        if span == 0:
            dst[0] = src[0]

    def expert_round(src, dst, sem, span):
        blocks = pl.ds(max(1, span * GROUP), (span + 1) * GROUP - max(1, span * GROUP))
        return pltpu.make_async_remote_copy(
            src_ref=src.at[blocks],
            dst_ref=dst.at[blocks],
            send_sem=sem.at[2 * span],
            recv_sem=sem.at[2 * span + 1],
            device_id=(g, e),
            device_id_type=MESH,
        )

    exchange(send_a, recv_a, a_sem, ndp, g, by_dp)

    spread_tok = (iota((ndp, ncol), 1) // Q == iota((ndp, ncol), 0)).astype(F32)
    names = mm(ids_ref[...].astype(F32), spread_tok)
    weights = mm(gates_ref[...], spread_tok, precision=HIGH)
    vcol[...] = names
    expert_row = lax.rem(iota((nexp, ncol), 0) + e, nexp).astype(F32)
    member = jnp.zeros((nexp, ncol), F32)
    weight = jnp.zeros((nexp, ncol), F32)
    for k in range(top):
        hit = names[k : k + 1, :] == expert_row
        member = jnp.where(hit, 1.0, member)
        weight = jnp.where(hit, weights[k : k + 1, :], weight)
    earlier = jnp.logical_and(
        iota((ncol, ncol), 0) // Q < iota((ncol, ncol), 1) // Q,
        lax.rem(iota((ncol, ncol), 0), Q) == 0,
    )
    rank = mm(member.astype(BF16), earlier.astype(F32).astype(BF16))
    slot_of = jnp.where(member > 0.0, rank, -1.0)
    cube = (nexp, J, ncol)
    slot3 = jnp.broadcast_to(slot_of[:, None, :], cube)
    weight3 = jnp.broadcast_to(weight[:, None, :], cube)
    jrow = iota((J, ncol), 0)
    quarter = lax.rem(iota((J, ncol), 1), Q)
    slot_j = lax.rem(jrow, SLOTS)
    used = jrow < 4 * SLOTS
    first = jrow < 2 * SLOTS
    same = jnp.logical_and(jrow // SLOTS == quarter, used)
    slot_want = jnp.where(same, slot_j, 99).astype(F32)[None]
    placed = slot3 == slot_want
    first3 = jnp.broadcast_to(first.astype(F32)[None], cube) > 0.0
    p_out = jnp.where(placed, jnp.where(first3, 1.0, weight3), 0.0).reshape(nexp * J, ncol)
    pd_hi[...], pd_lo[...] = split2(p_out)
    slots_kept[...] = slot_of
    weight_kept[...] = weight

    perm_shape = (4 * SLOTS * GROUP, GROUP * J)
    perm_row, perm_col = iota(perm_shape, 0), iota(perm_shape, 1)
    perm = jnp.logical_and(
        perm_row // GROUP == lax.rem(perm_col, J), lax.rem(perm_row, GROUP) == perm_col // J
    )
    perm = perm.astype(F32).astype(BF16)

    exchange_done(send_a, recv_a, a_sem, ndp, by_dp)
    mine = recv_a[...].reshape(ncol, LANES).astype(BF16)
    lines_of = [slice(span * GROUP * J, (span + 1) * GROUP * J) for span in range(parts)]
    for span in range(parts):
        sent = mm(pd_hi[lines_of[span]], mine) + mm(pd_lo[lines_of[span]], mine)
        send_b[span * GROUP : (span + 1) * GROUP] = sent.astype(BF16).reshape(GROUP, J, LANES)
        expert_start(send_b, recv_b, b_sem, span, 1)

    fields = [(j // (2 * SLOTS), j // SLOTS % 2, j % SLOTS) for j in range(4 * SLOTS)]

    def unpack(span):
        block = recv_b[span * GROUP : (span + 1) * GROUP].reshape(GROUP * J, LANES)
        sorted_rows = mm(perm, block).astype(BF16)
        for j, (kind, half, slot) in enumerate(fields):
            gath[
                g,
                span,
                kind,
                slot * GROUP : (slot + 1) * GROUP,
                half * LANES : (half + 1) * LANES,
            ] = sorted_rows[j * GROUP : (j + 1) * GROUP]

    def origin(direction, step, which):
        return at_z(-step if direction == 0 else step, which)

    def goes(direction, step, piece):
        return step < far or (step == far and piece // 2 == direction)

    def ring_copy(direction, step, piece):
        spot = gath.at[origin(direction, step, core), piece]
        return pltpu.make_async_remote_copy(
            src_ref=spot,
            dst_ref=spot,
            send_sem=ag_send.at[direction, step, piece],
            recv_sem=ag_recv.at[direction, step, piece],
            device_id=(toward[direction], e),
            device_id_type=MESH,
        )

    def arrival(direction, step, piece):
        spot = gath.at[origin(direction, step + 1, core), piece]
        return pltpu.make_async_remote_copy(
            src_ref=spot,
            dst_ref=spot,
            send_sem=ag_send.at[direction, step, piece],
            recv_sem=ag_recv.at[direction, step, piece],
            device_id=(toward[direction], e),
            device_id_type=MESH,
        )

    def sib_copy(direction, step, piece, which):
        spot = gath.at[origin(direction, step, which), piece]
        return pltpu.make_async_remote_copy(
            src_ref=spot,
            dst_ref=spot,
            send_sem=sibg_send.at[direction, step, piece],
            recv_sem=sibg_recv.at[direction, step, piece],
            device_id=(sibling, e),
            device_id_type=MESH,
        )

    for piece in range(parts):
        expert_round(send_b, recv_b, b_sem, piece).wait_recv()
        unpack(piece)
        for direction in range(2):
            if goes(direction, 1, piece):
                ring_copy(direction, 0, piece).start()
        sib_copy(0, 0, piece, core).start()

    slot3 = jnp.broadcast_to(slots_kept[...][:, None, :], cube)
    weight3 = jnp.broadcast_to(weight_kept[...][:, None, :], cube)
    placed = slot3 == slot_want
    p_back = jnp.where(placed, jnp.where(first3, weight3, 1.0), 0.0).reshape(nexp * J, ncol)
    pr_hi[...], pr_lo[...] = split2(p_back.T)
    cross = jnp.logical_and(jrow // SLOTS + 2 == quarter, first)
    cross_want = jnp.where(cross, slot_j, 99).astype(F32)[None]
    score_mask[...] = jnp.where(slot3 == cross_want, 1.0, 0.0).reshape(nexp * J, ncol)

    for step in range(1, far + 1):
        for piece in range(4):
            for direction in range(2):
                if goes(direction, step, piece):
                    arrival(direction, step - 1, piece).wait_recv()
                    if goes(direction, step + 1, piece):
                        ring_copy(direction, step, piece).start()
                    sib_copy(direction, step, piece, core).start()
    for piece in range(4):
        sib_copy(0, 0, piece, other).wait_recv()
    for step in range(1, far + 1):
        for piece in range(4):
            for direction in range(2):
                if goes(direction, step, piece):
                    sib_copy(direction, step, piece, other).wait_recv()

    for load in loads:
        load.wait()

    def held(block, kind):
        return jnp.concatenate([gath[block, piece, kind] for piece in range(parts)], axis=0)

    def columns(block):
        return pl.ds(pl.multiple_of(block * ds, ds), ds)

    pre = jnp.zeros((rows, 2 * ff), F32)
    back = jnp.zeros((rows, ff), F32)
    for block in range(ndp):
        pre += mm(held(block, 0), wgu[:, block * ds : (block + 1) * ds], 1, 1)
        back += mm(held(block, 1), wd[:, block * ds : (block + 1) * ds], 1, 1)
    gate_pre = pre[:, :ff]
    up_pre = pre[:, ff:]
    logistic = 1.0 / (1.0 + jnp.exp(-gate_pre))
    silu = gate_pre * logistic
    hidden = (silu * up_pre).astype(BF16)
    act_gate = back * up_pre * logistic * (1.0 + gate_pre * (1.0 - logistic))
    act_up = back * silu
    acts = jnp.concatenate([act_gate, act_up], axis=1).astype(BF16)

    def make_part(block):
        outs = (
            mm(hidden, wd[:, columns(block)]).astype(BF16),
            mm(acts, wgu[:, columns(block)]).astype(BF16),
        )
        for piece in range(parts):
            for kind in range(2):
                part[block, piece, kind] = outs[kind][piece * cut : (piece + 1) * cut]

    def pair_copy(place, which):
        return pltpu.make_async_remote_copy(
            src_ref=part.at[at_z(place, which)],
            dst_ref=sib_rx.at[at_z(place, 0) // 2],
            send_sem=sibr_send.at[place],
            recv_sem=sibr_recv.at[place],
            device_id=(sibling, e),
            device_id_type=MESH,
        )

    def make_parts(places):
        for place in places:
            make_part(at_z(place, other))
            pair_copy(place, other).start()
            make_part(at_z(place, core))

    def at_distance(away):
        return sorted({away, (nz - away) % nz})

    make_parts(at_distance(far))
    make_parts(at_distance(far - 1))

    def chain_copy(direction, step, piece):
        return pltpu.make_async_remote_copy(
            src_ref=ring_tx.at[direction, step, piece],
            dst_ref=ring_rx.at[direction, step, piece],
            send_sem=rs_send.at[direction, step, piece],
            recv_sem=rs_recv.at[direction, step, piece],
            device_id=(toward[direction], e),
            device_id_type=MESH,
        )

    def chip_sum(place, piece):
        return part[at_z(place, core), piece].astype(F32) + sib_rx[
            at_z(place, 0) // 2, piece
        ].astype(F32)

    def weight_grads(blocks):
        for block in blocks:
            cols = slice(block * ds, (block + 1) * ds)
            gu_out[:, cols] = mm(acts, held(block, 0), 0, 0).astype(BF16)
            d_out[:, cols] = mm(hidden, held(block, 1), 0, 0).astype(BF16)

    turns = (
        [(0, 0), (0, 1), (1, 2), (1, 3), (1, 0), (1, 1), (2, 2), (2, 0), (2, 1), (2, 3)]
        + [(3, 0), (3, 1), (3, 2), (3, 3)],
        [(0, 2), (0, 3)] + [(step, piece) for step in range(1, far) for piece in range(4)],
    )
    count = len(turns[0])
    paired = set()
    made = far - 1
    done_blocks = 0
    for turn in range(count):
        for direction in range(2):
            step, piece = turns[direction][turn]
            away = far - step
            place = away if direction == 0 else (nz - away) % nz
            if place not in paired:
                pair_copy(place, other).wait_recv()
                paired.add(place)
            total = chip_sum(place, piece)
            if step > (0 if piece // 2 == direction else 1):
                chain_copy(direction, step - 1, piece).wait_recv()
                total += ring_rx[direction, step - 1, piece].astype(F32)
            ring_tx[direction, step, piece] = total.astype(BF16)
            chain_copy(direction, step, piece).start()
        if turn % 3 == 2 and made > 0:
            made -= 1
            make_parts(at_distance(made))
        elif turn > 2:
            weight_grads(range(done_blocks, min(ndp, done_blocks + 2)))
            done_blocks = min(ndp, done_blocks + 2)
    weight_grads(range(done_blocks, ndp))
    stores = [
        pltpu.make_async_copy(gu_out.at[pl.ds(0, ff)], wgg_ref.at[0], o_sem.at[0]),
        pltpu.make_async_copy(gu_out.at[pl.ds(ff, ff)], wug_ref.at[0], o_sem.at[1]),
        pltpu.make_async_copy(d_out, wdg_ref.at[0], o_sem.at[2]),
    ]
    for store in stores:
        store.start()
    pair_copy(0, other).wait_recv()
    unperm_shape = (GROUP * J, 4 * SLOTS * GROUP)
    un_row, un_col = iota(unperm_shape, 0), iota(unperm_shape, 1)
    unperm = jnp.logical_and(
        un_col // GROUP == lax.rem(un_row, J), lax.rem(un_col, GROUP) == un_row // J
    )
    unperm = unperm.astype(F32).astype(BF16)
    for piece in range(parts):
        total = chip_sum(0, piece)
        for direction in range(2):
            chain_copy(direction, far - 1, piece).wait_recv()
            total += ring_rx[direction, far - 1, piece].astype(F32)
        final = total.astype(BF16)
        taken = [
            final[kind, slot * GROUP : (slot + 1) * GROUP, half * LANES : (half + 1) * LANES]
            for kind, half, slot in fields
        ]
        block = mm(unperm, jnp.concatenate(taken, axis=0)).astype(BF16)
        send_c[piece * GROUP : (piece + 1) * GROUP] = block.reshape(GROUP, J, LANES)
        expert_start(send_c, recv_c, c_sem, piece, -1)

    result = jnp.zeros((ncol, LANES), F32)
    mine = recv_a[...].reshape(ncol, LANES).astype(BF16)
    by_span = []
    for span in range(parts):
        expert_round(send_c, recv_c, c_sem, span).wait_recv()
        came = recv_c[span * GROUP : (span + 1) * GROUP].reshape(GROUP * J, LANES)
        lines = lines_of[span]
        result += mm(pr_hi[:, lines], came) + mm(pr_lo[:, lines], came)
        products = mm(came, mine, 1, 1) * score_mask[lines]
        by_span.append(jnp.sum(products.reshape(GROUP, J, ncol), axis=1))
    per_expert = jnp.concatenate(by_span, axis=0)
    names = vcol[...]
    expert_row = lax.rem(iota((nexp, ncol), 0) + e, nexp).astype(F32)
    scores = [
        jnp.sum(jnp.where(names[k : k + 1, :] == expert_row, per_expert, 0.0), axis=0, keepdims=True)
        for k in range(top)
    ]
    scores = jnp.concatenate(scores + [jnp.zeros((LANES - top, ncol), F32)], axis=0)
    pick = jnp.logical_and(
        iota((ncol, ncol), 0) // Q == iota((ncol, ncol), 1) // Q,
        lax.rem(iota((ncol, ncol), 0), Q) == 4,
    ).astype(F32)
    result += mm(pick, scores, 1, 1, HIGH)
    send_d[...] = result.reshape(ndp, Q, LANES)
    exchange(send_d, recv_d, d_sem, ndp, g, by_dp)
    exchange_done(send_d, recv_d, d_sem, ndp, by_dp)
    out_cols, grad_cols = [], []
    total = jnp.zeros((1, LANES), F32)
    for came_from in range(ndp):
        for half in range(2):
            out_cols.append(recv_d[came_from, half : half + 1, :])
            grad_cols.append(recv_d[came_from, 2 + half : 3 + half, :])
        total += recv_d[came_from, 4:5, :]
    mixed_ref[...] = jnp.concatenate(out_cols, axis=1).astype(BF16)
    tgrad_ref[...] = jnp.concatenate(grad_cols, axis=1).astype(BF16)
    ggrad_ref[...] = total[:, :top]

    for span in range(parts):
        expert_round(send_b, recv_b, b_sem, span).wait_send()
        expert_round(send_c, recv_c, c_sem, span).wait_send()
    for piece in range(4):
        sib_copy(0, 0, piece, core).wait_send()
    for step in range(far + 1):
        for piece in range(4):
            for direction in range(2):
                if step < far and goes(direction, step + 1, piece):
                    ring_copy(direction, step, piece).wait_send()
                if step > 0 and goes(direction, step, piece):
                    sib_copy(direction, step, piece, core).wait_send()
                if step < far and (step > 0 or piece // 2 == direction):
                    chain_copy(direction, step, piece).wait_send()
    for place in range(nz):
        pair_copy(place, other).wait_send()
    for store in stores:
        store.wait()


def on_device(tokens, expert_ids, gates, w_gate, w_up, w_down, cotangent):
    ndp, nexp = lax.axis_size("dp"), lax.axis_size("expert")
    nz, far = ndp // 2, ndp // 4
    ff, width = w_down.shape[1:]
    rows = SLOTS * nexp
    cut, ds, ncol = SLOTS * GROUP, 2 * LANES, ndp * Q
    vmem, hbm = pl.BlockSpec(memory_space=pltpu.VMEM), pl.BlockSpec(memory_space=pl.ANY)
    row = jax.ShapeDtypeStruct(tokens.shape, BF16)
    weight = jax.ShapeDtypeStruct(w_down.shape, BF16)
    dma = pltpu.SemaphoreType.DMA
    outs = pl.pallas_call(
        functools.partial(kernel, ndp, nexp),
        out_shape=(
            row,
            row,
            jax.ShapeDtypeStruct((1, expert_ids.shape[1]), F32),
            weight,
            weight,
            weight,
        ),
        in_specs=[pl.BlockSpec(memory_space=pltpu.HBM)] * 7,
        out_specs=(vmem, vmem, vmem, hbm, hbm, hbm),
        scratch_shapes=[
            pltpu.VMEM(tokens.shape, BF16),
            pltpu.VMEM(tokens.shape, BF16),
            pltpu.VMEM(expert_ids.shape[::-1], jnp.int32),
            pltpu.VMEM(expert_ids.shape[::-1], F32),
            pltpu.VMEM((2 * ff, width), BF16),
            pltpu.VMEM((ff, width), BF16),
            pltpu.VMEM((2 * ff, width), BF16),
            pltpu.VMEM((ff, width), BF16),
            pltpu.VMEM((ndp, Q, LANES), F32),
            pltpu.VMEM((ndp, Q, LANES), F32),
            pltpu.VMEM((nexp, J, LANES), BF16),
            pltpu.VMEM((nexp, J, LANES), BF16),
            pltpu.VMEM((ndp, nexp // GROUP, 2, cut, ds), BF16),
            pltpu.VMEM((ndp, nexp // GROUP, 2, cut, ds), BF16),
            pltpu.VMEM((nz, nexp // GROUP, 2, cut, ds), BF16),
            pltpu.VMEM((2, far, 4, 2, cut, ds), BF16),
            pltpu.VMEM((2, far, 4, 2, cut, ds), BF16),
            pltpu.VMEM((nexp, J, LANES), BF16),
            pltpu.VMEM((nexp, J, LANES), BF16),
            pltpu.VMEM((ndp, Q, LANES), F32),
            pltpu.VMEM((ndp, Q, LANES), F32),
            pltpu.VMEM((nexp * J, ncol), BF16),
            pltpu.VMEM((nexp * J, ncol), BF16),
            pltpu.VMEM((ncol, nexp * J), BF16),
            pltpu.VMEM((ncol, nexp * J), BF16),
            pltpu.VMEM((nexp * J, ncol), F32),
            pltpu.VMEM((expert_ids.shape[1], ncol), F32),
            pltpu.VMEM((nexp, ncol), F32),
            pltpu.VMEM((nexp, ncol), F32),
            dma((4,)),
            dma((3,)),
            dma((3,)),
            dma((2,)),
            dma((2 * nexp // GROUP,)),
            dma((2 * nexp // GROUP,)),
            dma((2,)),
            dma((2, far, 4)),
            dma((2, far, 4)),
            dma((2, far + 1, 4)),
            dma((2, far + 1, 4)),
            dma((nz,)),
            dma((nz,)),
            dma((2, far, 4)),
            dma((2, far, 4)),
        ],
        compiler_params=pltpu.CompilerParams(
            collective_id=0, has_side_effects=True, vmem_limit_bytes=61 * 1024 * 1024
        ),
        cost_estimate=pl.CostEstimate(
            flops=18 * rows * ff * width, bytes_accessed=6 * ff * width * 2, transcendentals=rows * ff
        ),
    )(tokens, cotangent, expert_ids.T, gates.T, w_gate, w_up, w_down)
    return pl.pallas_call(
        copy_out,
        out_shape=[jax.ShapeDtypeStruct(out.shape, out.dtype) for out in outs],
        in_specs=[pl.BlockSpec(memory_space=pltpu.HBM)] * 6,
        out_specs=[pl.BlockSpec(memory_space=pltpu.HBM)] * 6,
        scratch_shapes=[pltpu.VMEM(out.shape, out.dtype) for out in outs] + [dma((3 * CHUNKS + 3,)), dma((3 * CHUNKS + 3,))],
        compiler_params=pltpu.CompilerParams(vmem_limit_bytes=61 * 1024 * 1024),
    )(*outs)


def copy_out(*refs):
    count = len(refs) // 3
    sources, targets, held = refs[:count], refs[count : 2 * count], refs[2 * count : 3 * count]
    in_sem, out_sem = refs[3 * count :]
    chunks = []
    for i in range(count)[::-1]:
        if len(sources[i].shape) == 3:
            size = sources[i].shape[1] // CHUNKS
            chunks += [(i, pl.ds(c * size, size)) for c in range(CHUNKS)]
        else:
            chunks.append((i, None))

    def move(source, target, sem, place):
        if place is None:
            return pltpu.make_async_copy(source, target, sem)
        return pltpu.make_async_copy(source.at[:, place], target.at[:, place], sem)

    gets = [move(sources[i], held[i], in_sem.at[n], p) for n, (i, p) in enumerate(chunks)]
    puts = [move(held[i], targets[i], out_sem.at[n], p) for n, (i, p) in enumerate(chunks)]
    for get in gets:
        get.start()
    for get, put in zip(gets, puts):
        get.wait()
        put.start()
    for put in puts:
        put.wait()


def solution(mesh):
    placed = (
        P(("expert", "dp"), None),
        P("expert", None),
        P("expert", None),
        P("expert", "dp", None),
        P("expert", "dp", None),
        P("expert", "dp", None),
        P(("expert", "dp"), None),
    )
    return jax.shard_map(
        on_device,
        mesh=mesh,
        in_specs=placed,
        out_specs=(
            P(("expert", "dp"), None),
            P(("expert", "dp"), None),
            P(("expert", "dp"), None),
            P("expert", "dp", None),
            P("expert", "dp", None),
            P("expert", "dp", None),
        ),
        check_vma=False,
    )
```

```python
import functools

import jax
import jax.numpy as jnp
from jax import lax
from jax.experimental import pallas as pl
from jax.experimental.pallas import tpu as pltpu
from jax.sharding import PartitionSpec as P

F32 = jnp.float32
BF16 = jnp.bfloat16
MESH = pl.DeviceIdType.MESH
SLOTS = 3
LANES = 128
Q = 8
J = 16
GROUP = 16
CHUNKS = 4
HIGH = lax.Precision.HIGHEST


def mm(left, right, left_dim=1, right_dim=0, precision=None):
    return lax.dot_general(
        left,
        right,
        (((left_dim,), (right_dim,)), ((), ())),
        preferred_element_type=F32,
        precision=precision,
    )


def iota(shape, dim):
    return lax.broadcasted_iota(jnp.int32, shape, dim)


def split2(value):
    high = value.astype(BF16)
    return high, (value - high.astype(F32)).astype(BF16)


def kernel(
    ndp,
    nexp,
    tok_hbm,
    cot_hbm,
    ids_hbm,
    gates_hbm,
    wg_ref,
    wu_ref,
    wd_ref,
    mixed_ref,
    tgrad_ref,
    ggrad_ref,
    wgg_ref,
    wug_ref,
    wdg_ref,
    tok_ref,
    cot_ref,
    ids_ref,
    gates_ref,
    wgu,
    wd,
    gu_out,
    d_out,
    send_a,
    recv_a,
    send_b,
    recv_b,
    send_f,
    recv_f,
    gath,
    part,
    sib_rx,
    ring_tx,
    ring_rx,
    send_c,
    recv_c,
    send_h,
    recv_h,
    send_d,
    recv_d,
    pd_hi,
    pd_lo,
    pr_hi,
    pr_lo,
    score_mask,
    vcol,
    slots_kept,
    weight_kept,
    i_sem,
    w_sem,
    o_sem,
    a_sem,
    b_sem,
    f_sem,
    c_sem,
    h_sem,
    d_sem,
    ag_send,
    ag_recv,
    sibg_send,
    sibg_recv,
    sibr_send,
    sibr_recv,
    rs_send,
    rs_recv,
):
    g = lax.axis_index("dp")
    e = lax.axis_index("expert")
    nz = ndp // 2
    far = nz // 2
    z = g // 2
    core = lax.rem(g, 2)
    other = 1 - core
    rows = SLOTS * nexp
    cut = SLOTS * GROUP
    parts = nexp // GROUP
    ff = wd.shape[0]
    ncol = ndp * Q
    ds = 2 * LANES
    top = ids_ref.shape[0]

    def at_z(offset, which):
        return lax.rem(z + offset + nz, nz) * 2 + which

    right = at_z(1, core)
    left = at_z(-1, core)
    sibling = z * 2 + other
    toward = (right, left)

    small = [
        pltpu.make_async_copy(tok_hbm, tok_ref, i_sem.at[0]),
        pltpu.make_async_copy(cot_hbm, cot_ref, i_sem.at[1]),
        pltpu.make_async_copy(ids_hbm, ids_ref, i_sem.at[2]),
        pltpu.make_async_copy(gates_hbm, gates_ref, i_sem.at[3]),
    ]
    for load in small:
        load.start()

    barrier = pltpu.get_barrier_semaphore()

    def greet_dp(i, carry):
        pl.semaphore_signal(
            barrier, inc=1, device_id=(lax.rem(g + i, ndp), e), device_id_type=MESH
        )
        return carry

    def greet_expert(i, carry):
        pl.semaphore_signal(
            barrier, inc=1, device_id=(g, lax.rem(e + i, nexp)), device_id_type=MESH
        )
        return carry

    lax.fori_loop(1, ndp, greet_dp, 0)
    lax.fori_loop(1, nexp, greet_expert, 0)

    loads = [
        pltpu.make_async_copy(wg_ref.at[0], wgu.at[pl.ds(0, ff)], w_sem.at[0]),
        pltpu.make_async_copy(wu_ref.at[0], wgu.at[pl.ds(ff, ff)], w_sem.at[1]),
        pltpu.make_async_copy(wd_ref.at[0], wd, w_sem.at[2]),
    ]
    for load in loads:
        load.start()

    for load in small:
        load.wait()
    token = tok_ref[...].astype(F32)
    cotan = cot_ref[...].astype(F32)
    for to in range(ndp):
        for half in range(2):
            lane = to * ds + half * LANES
            send_a[to, half : half + 1, :] = token[:, lane : lane + LANES]
            send_a[to, 2 + half : 3 + half, :] = cotan[:, lane : lane + LANES]
            send_a[(to + ndp // 2) % ndp, 4 + half : 5 + half, :] = token[:, lane : lane + LANES]
            send_a[(to + ndp // 2) % ndp, 6 + half : 7 + half, :] = cotan[:, lane : lane + LANES]

    pl.semaphore_wait(barrier, ndp - 1 + nexp - 1)

    def exchange(src, dst, sem, count, me, peer_id):
        def start(i, carry):
            peer = lax.rem(me + i, count)
            pltpu.make_async_remote_copy(
                src_ref=src.at[peer],
                dst_ref=dst.at[me],
                send_sem=sem.at[0],
                recv_sem=sem.at[1],
                device_id=peer_id(peer),
                device_id_type=MESH,
            ).start()
            return carry

        lax.fori_loop(1, count, start, 0)
        dst[me] = src[me]

    def exchange_done(src, dst, sem, count, peer_id):
        done = pltpu.make_async_remote_copy(
            src_ref=src.at[pl.ds(0, count - 1)],
            dst_ref=dst.at[pl.ds(0, count - 1)],
            send_sem=sem.at[0],
            recv_sem=sem.at[1],
            device_id=peer_id(0),
            device_id_type=MESH,
        )
        done.wait_recv()
        done.wait_send()

    def by_dp(peer):
        return (peer, e)

    def expert_start(src, dst, sem, span, way):
        def start(i, carry):
            pltpu.make_async_remote_copy(
                src_ref=src.at[i],
                dst_ref=dst.at[i],
                send_sem=sem.at[2 * span],
                recv_sem=sem.at[2 * span + 1],
                device_id=(g, lax.rem(e + way * i + nexp, nexp)),
                device_id_type=MESH,
            ).start()
            return carry

        lax.fori_loop(max(1, span * GROUP), (span + 1) * GROUP, start, 0)
        if span == 0:
            dst[0] = src[0]

    def expert_round(src, dst, sem, span):
        blocks = pl.ds(max(1, span * GROUP), (span + 1) * GROUP - max(1, span * GROUP))
        return pltpu.make_async_remote_copy(
            src_ref=src.at[blocks],
            dst_ref=dst.at[blocks],
            send_sem=sem.at[2 * span],
            recv_sem=sem.at[2 * span + 1],
            device_id=(g, e),
            device_id_type=MESH,
        )

    exchange(send_a, recv_a, a_sem, ndp, g, by_dp)

    spread_tok = (iota((ndp, ncol), 1) // Q == iota((ndp, ncol), 0)).astype(F32)
    names = mm(ids_ref[...].astype(F32), spread_tok)
    weights = mm(gates_ref[...], spread_tok, precision=HIGH)
    vcol[...] = names
    expert_row = lax.rem(iota((nexp, ncol), 0) + e, nexp).astype(F32)
    member = jnp.zeros((nexp, ncol), F32)
    weight = jnp.zeros((nexp, ncol), F32)
    for k in range(top):
        hit = names[k : k + 1, :] == expert_row
        member = jnp.where(hit, 1.0, member)
        weight = jnp.where(hit, weights[k : k + 1, :], weight)
    earlier = jnp.logical_and(
        iota((ncol, ncol), 0) // Q < iota((ncol, ncol), 1) // Q,
        lax.rem(iota((ncol, ncol), 0), Q) == 0,
    )
    rank = mm(member.astype(BF16), earlier.astype(F32).astype(BF16))
    slot_of = jnp.where(member > 0.0, rank, -1.0)
    cube = (nexp, J, ncol)
    slot3 = jnp.broadcast_to(slot_of[:, None, :], cube)
    weight3 = jnp.broadcast_to(weight[:, None, :], cube)
    jrow = iota((J, ncol), 0)
    quarter = lax.rem(iota((J, ncol), 1), Q)
    slot_j = lax.rem(jrow, SLOTS)
    used = jrow < 4 * SLOTS
    first = jrow < 2 * SLOTS
    same = jnp.logical_and(jrow // SLOTS == quarter, used)
    slot_want = jnp.where(same, slot_j, 99).astype(F32)[None]
    placed = slot3 == slot_want
    first3 = jnp.broadcast_to(first.astype(F32)[None], cube) > 0.0
    p_out = jnp.where(placed, jnp.where(first3, 1.0, weight3), 0.0).reshape(nexp * J, ncol)
    pd_hi[...], pd_lo[...] = split2(p_out)
    slots_kept[...] = slot_of
    weight_kept[...] = weight

    perm_shape = (4 * SLOTS * GROUP, GROUP * J)
    perm_row, perm_col = iota(perm_shape, 0), iota(perm_shape, 1)
    perm = jnp.logical_and(
        perm_row // GROUP == lax.rem(perm_col, J), lax.rem(perm_row, GROUP) == perm_col // J
    )
    perm = perm.astype(F32).astype(BF16)

    exchange_done(send_a, recv_a, a_sem, ndp, by_dp)
    mine = recv_a[...].reshape(ncol, LANES).astype(BF16)
    lines_of = [slice(span * GROUP * J, (span + 1) * GROUP * J) for span in range(parts)]
    for span in range(parts):
        sent = mm(pd_hi[lines_of[span]], mine) + mm(pd_lo[lines_of[span]], mine)
        send_b[span * GROUP : (span + 1) * GROUP] = sent.astype(BF16).reshape(GROUP, J, LANES)
        expert_start(send_b, recv_b, b_sem, span, 1)
    across = recv_a[...]
    across = jnp.concatenate([across[:, Q // 2 :], across[:, : Q // 2]], axis=1)
    across = across.reshape(ncol, LANES).astype(BF16)

    def send_across(span):
        sent = mm(pd_hi[lines_of[span]], across) + mm(pd_lo[lines_of[span]], across)
        send_f[span * GROUP : (span + 1) * GROUP] = sent.astype(BF16).reshape(GROUP, J, LANES)
        expert_start(send_f, recv_f, f_sem, span, 1)

    fields = [(j // (2 * SLOTS), j // SLOTS % 2, j % SLOTS) for j in range(4 * SLOTS)]

    def unpack(span, arrived, where):
        block = arrived[span * GROUP : (span + 1) * GROUP].reshape(GROUP * J, LANES)
        sorted_rows = mm(perm, block).astype(BF16)
        for j, (kind, half, slot) in enumerate(fields):
            gath[
                where,
                span,
                kind,
                slot * GROUP : (slot + 1) * GROUP,
                half * LANES : (half + 1) * LANES,
            ] = sorted_rows[j * GROUP : (j + 1) * GROUP]

    def origin(direction, step, which):
        return at_z(-step if direction == 0 else step, which)

    def goes(direction, step, piece):
        return step < far or (step == far and piece // 2 == direction)

    def ring_copy(direction, step, piece):
        spot = gath.at[origin(direction, step, core), piece]
        return pltpu.make_async_remote_copy(
            src_ref=spot,
            dst_ref=spot,
            send_sem=ag_send.at[direction, step, piece],
            recv_sem=ag_recv.at[direction, step, piece],
            device_id=(toward[direction], e),
            device_id_type=MESH,
        )

    def arrival(direction, step, piece):
        spot = gath.at[origin(direction, step + 1, core), piece]
        return pltpu.make_async_remote_copy(
            src_ref=spot,
            dst_ref=spot,
            send_sem=ag_send.at[direction, step, piece],
            recv_sem=ag_recv.at[direction, step, piece],
            device_id=(toward[direction], e),
            device_id_type=MESH,
        )

    def sib_copy(direction, step, piece, which):
        spot = gath.at[origin(direction, step, which), piece]
        return pltpu.make_async_remote_copy(
            src_ref=spot,
            dst_ref=spot,
            send_sem=sibg_send.at[direction, step, piece],
            recv_sem=sibg_recv.at[direction, step, piece],
            device_id=(sibling, e),
            device_id_type=MESH,
        )

    for piece in range(parts):
        expert_round(send_b, recv_b, b_sem, piece).wait_recv()
        unpack(piece, recv_b, g)
        for direction in range(2):
            ring_copy(direction, 0, piece).start()
        sib_copy(0, 0, piece, core).start()
        send_across(piece)

    slot3 = jnp.broadcast_to(slots_kept[...][:, None, :], cube)
    weight3 = jnp.broadcast_to(weight_kept[...][:, None, :], cube)
    placed = slot3 == slot_want
    p_back = jnp.where(placed, jnp.where(first3, weight3, 1.0), 0.0).reshape(nexp * J, ncol)
    pr_hi[...], pr_lo[...] = split2(p_back.T)
    cross = jnp.logical_and(jrow // SLOTS + 2 == quarter, first)
    cross_want = jnp.where(cross, slot_j, 99).astype(F32)[None]
    score_mask[...] = jnp.where(slot3 == cross_want, 1.0, 0.0).reshape(nexp * J, ncol)

    for step in range(1, far):
        for piece in range(4):
            for direction in range(2):
                arrival(direction, step - 1, piece).wait_recv()
                if step + 1 < far:
                    ring_copy(direction, step, piece).start()
                sib_copy(direction, step, piece, core).start()
            if step == far - 1:
                expert_round(send_f, recv_f, f_sem, piece).wait_recv()
                unpack(piece, recv_f, at_z(far, core))
                sib_copy(piece // 2, far, piece, core).start()
    for piece in range(4):
        sib_copy(0, 0, piece, other).wait_recv()
    for step in range(1, far + 1):
        for piece in range(4):
            for direction in range(2):
                if goes(direction, step, piece):
                    sib_copy(direction, step, piece, other).wait_recv()

    for load in loads:
        load.wait()

    def held(block, kind):
        return jnp.concatenate([gath[block, piece, kind] for piece in range(parts)], axis=0)

    def columns(block):
        return pl.ds(pl.multiple_of(block * ds, ds), ds)

    pre = jnp.zeros((rows, 2 * ff), F32)
    back = jnp.zeros((rows, ff), F32)
    for block in range(ndp):
        pre += mm(held(block, 0), wgu[:, block * ds : (block + 1) * ds], 1, 1)
        back += mm(held(block, 1), wd[:, block * ds : (block + 1) * ds], 1, 1)
    gate_pre = pre[:, :ff]
    up_pre = pre[:, ff:]
    logistic = 1.0 / (1.0 + jnp.exp(-gate_pre))
    silu = gate_pre * logistic
    hidden = (silu * up_pre).astype(BF16)
    act_gate = back * up_pre * logistic * (1.0 + gate_pre * (1.0 - logistic))
    act_up = back * silu
    acts = jnp.concatenate([act_gate, act_up], axis=1).astype(BF16)

    def make_part(block):
        outs = (
            mm(hidden, wd[:, columns(block)]).astype(BF16),
            mm(acts, wgu[:, columns(block)]).astype(BF16),
        )
        for piece in range(parts):
            for kind in range(2):
                part[block, piece, kind] = outs[kind][piece * cut : (piece + 1) * cut]

    def pair_copy(place, which):
        return pltpu.make_async_remote_copy(
            src_ref=part.at[at_z(place, which)],
            dst_ref=sib_rx.at[at_z(place, 0) // 2],
            send_sem=sibr_send.at[place],
            recv_sem=sibr_recv.at[place],
            device_id=(sibling, e),
            device_id_type=MESH,
        )

    def make_parts(places):
        for place in places:
            make_part(at_z(place, other))
            pair_copy(place, other).start()
            make_part(at_z(place, core))

    def at_distance(away):
        return sorted({away, (nz - away) % nz})

    make_parts(at_distance(far - 1))

    def chain_copy(direction, step, piece):
        return pltpu.make_async_remote_copy(
            src_ref=ring_tx.at[direction, step, piece],
            dst_ref=ring_rx.at[direction, step, piece],
            send_sem=rs_send.at[direction, step, piece],
            recv_sem=rs_recv.at[direction, step, piece],
            device_id=(toward[direction], e),
            device_id_type=MESH,
        )

    def chip_sum(place, piece):
        return part[at_z(place, core), piece].astype(F32) + sib_rx[
            at_z(place, 0) // 2, piece
        ].astype(F32)

    def weight_grads(blocks):
        for block in blocks:
            cols = slice(block * ds, (block + 1) * ds)
            gu_out[:, cols] = mm(acts, held(block, 0), 0, 0).astype(BF16)
            d_out[:, cols] = mm(hidden, held(block, 1), 0, 0).astype(BF16)

    unperm_shape = (GROUP * J, 4 * SLOTS * GROUP)
    un_row, un_col = iota(unperm_shape, 0), iota(unperm_shape, 1)
    unperm = jnp.logical_and(
        un_col // GROUP == lax.rem(un_row, J), lax.rem(un_col, GROUP) == un_row // J
    )
    unperm = unperm.astype(F32).astype(BF16)

    def send_home(total, src, dst, sem, piece):
        final = total.astype(BF16)
        taken = [
            final[kind, slot * GROUP : (slot + 1) * GROUP, half * LANES : (half + 1) * LANES]
            for kind, half, slot in fields
        ]
        block = mm(unperm, jnp.concatenate(taken, axis=0)).astype(BF16)
        src[piece * GROUP : (piece + 1) * GROUP] = block.reshape(GROUP, J, LANES)
        expert_start(src, dst, sem, piece, -1)

    turns = [(step, piece) for step in range(1, far) for piece in range(4)]
    paired = set()
    done_blocks = 0
    for turn, (step, piece) in enumerate(turns):
        for direction in range(2):
            away = far - step
            place = away if direction == 0 else nz - away
            if place not in paired:
                pair_copy(place, other).wait_recv()
                paired.add(place)
            total = chip_sum(place, piece)
            if step > 1:
                chain_copy(direction, step - 1, piece).wait_recv()
                total += ring_rx[direction, step - 1, piece].astype(F32)
            ring_tx[direction, step, piece] = total.astype(BF16)
            chain_copy(direction, step, piece).start()
        if turn == 3:
            make_parts(at_distance(far))
            make_parts(at_distance(far - 2))
            pair_copy(far, other).wait_recv()
            for across_piece in range(parts):
                send_home(chip_sum(far, across_piece), send_h, recv_h, h_sem, across_piece)
        elif turn == 5:
            make_parts(at_distance(far - 3))
        elif turn == 7:
            make_parts(at_distance(0))
        elif turn > 3:
            weight_grads(range(done_blocks, min(ndp, done_blocks + 3)))
            done_blocks = min(ndp, done_blocks + 3)
    weight_grads(range(done_blocks, ndp))
    stores = [
        pltpu.make_async_copy(gu_out.at[pl.ds(0, ff)], wgg_ref.at[0], o_sem.at[0]),
        pltpu.make_async_copy(gu_out.at[pl.ds(ff, ff)], wug_ref.at[0], o_sem.at[1]),
        pltpu.make_async_copy(d_out, wdg_ref.at[0], o_sem.at[2]),
    ]
    for store in stores:
        store.start()
    pair_copy(0, other).wait_recv()
    for piece in range(parts):
        total = chip_sum(0, piece)
        for direction in range(2):
            chain_copy(direction, far - 1, piece).wait_recv()
            total += ring_rx[direction, far - 1, piece].astype(F32)
        send_home(total, send_c, recv_c, c_sem, piece)

    result = jnp.zeros((ncol, LANES), F32)
    mine = recv_a[...].reshape(ncol, LANES).astype(BF16)
    result_far = jnp.zeros((ncol, LANES), F32)
    across = recv_a[...]
    across = jnp.concatenate([across[:, Q // 2 :], across[:, : Q // 2]], axis=1)
    across = across.reshape(ncol, LANES).astype(BF16)
    by_span = []
    for span in range(parts):
        expert_round(send_h, recv_h, h_sem, span).wait_recv()
        came = recv_h[span * GROUP : (span + 1) * GROUP].reshape(GROUP * J, LANES)
        lines = lines_of[span]
        result_far += mm(pr_hi[:, lines], came) + mm(pr_lo[:, lines], came)
        products = mm(came, across, 1, 1) * score_mask[lines]
        by_span.append(jnp.sum(products.reshape(GROUP, J, ncol), axis=1))
    far_scores = jnp.concatenate(by_span, axis=0)
    by_span = []
    for span in range(parts):
        expert_round(send_c, recv_c, c_sem, span).wait_recv()
        came = recv_c[span * GROUP : (span + 1) * GROUP].reshape(GROUP * J, LANES)
        lines = lines_of[span]
        result += mm(pr_hi[:, lines], came) + mm(pr_lo[:, lines], came)
        products = mm(came, mine, 1, 1) * score_mask[lines]
        by_span.append(jnp.sum(products.reshape(GROUP, J, ncol), axis=1))
    per_expert = jnp.concatenate(by_span, axis=0) + far_scores
    names = vcol[...]
    expert_row = lax.rem(iota((nexp, ncol), 0) + e, nexp).astype(F32)
    scores = [
        jnp.sum(jnp.where(names[k : k + 1, :] == expert_row, per_expert, 0.0), axis=0, keepdims=True)
        for k in range(top)
    ]
    scores = jnp.concatenate(scores + [jnp.zeros((LANES - top, ncol), F32)], axis=0)
    pick = jnp.logical_and(
        iota((ncol, ncol), 0) // Q == iota((ncol, ncol), 1) // Q,
        lax.rem(iota((ncol, ncol), 0), Q) == 0,
    ).astype(F32)
    result_far = result_far.reshape(ndp, Q, LANES)
    result_far = jnp.concatenate([result_far[:, Q // 2 :], result_far[:, : Q // 2]], axis=1)
    send_d[:, :Q] = result.reshape(ndp, Q, LANES) + result_far
    send_d[:, Q:] = mm(pick, scores, 1, 1, HIGH).reshape(ndp, Q, LANES)
    exchange(send_d, recv_d, d_sem, ndp, g, by_dp)
    exchange_done(send_d, recv_d, d_sem, ndp, by_dp)
    out_cols, grad_cols = [], []
    total = jnp.zeros((1, LANES), F32)
    for came_from in range(ndp):
        for half in range(2):
            facing = (came_from + ndp // 2) % ndp
            out_cols.append(
                recv_d[came_from, half : half + 1, :] + recv_d[facing, 4 + half : 5 + half, :]
            )
            grad_cols.append(
                recv_d[came_from, 2 + half : 3 + half, :] + recv_d[facing, 6 + half : 7 + half, :]
            )
        total += recv_d[came_from, Q : Q + 1, :]
    mixed_ref[...] = jnp.concatenate(out_cols, axis=1).astype(BF16)
    tgrad_ref[...] = jnp.concatenate(grad_cols, axis=1).astype(BF16)
    ggrad_ref[...] = total[:, :top]

    for span in range(parts):
        expert_round(send_b, recv_b, b_sem, span).wait_send()
        expert_round(send_f, recv_f, f_sem, span).wait_send()
        expert_round(send_c, recv_c, c_sem, span).wait_send()
        expert_round(send_h, recv_h, h_sem, span).wait_send()
    for piece in range(4):
        sib_copy(0, 0, piece, core).wait_send()
    for step in range(far + 1):
        for piece in range(4):
            for direction in range(2):
                if step < far - 1:
                    ring_copy(direction, step, piece).wait_send()
                if step > 0 and goes(direction, step, piece):
                    sib_copy(direction, step, piece, core).wait_send()
                if 0 < step < far:
                    chain_copy(direction, step, piece).wait_send()
    for place in range(nz):
        pair_copy(place, other).wait_send()
    for store in stores:
        store.wait()


def on_device(tokens, expert_ids, gates, w_gate, w_up, w_down, cotangent):
    ndp, nexp = lax.axis_size("dp"), lax.axis_size("expert")
    nz, far = ndp // 2, ndp // 4
    ff, width = w_down.shape[1:]
    rows = SLOTS * nexp
    cut, ds, ncol = SLOTS * GROUP, 2 * LANES, ndp * Q
    vmem, hbm = pl.BlockSpec(memory_space=pltpu.VMEM), pl.BlockSpec(memory_space=pl.ANY)
    row = jax.ShapeDtypeStruct(tokens.shape, BF16)
    weight = jax.ShapeDtypeStruct(w_down.shape, BF16)
    dma = pltpu.SemaphoreType.DMA
    outs = pl.pallas_call(
        functools.partial(kernel, ndp, nexp),
        out_shape=(
            row,
            row,
            jax.ShapeDtypeStruct((1, expert_ids.shape[1]), F32),
            weight,
            weight,
            weight,
        ),
        in_specs=[pl.BlockSpec(memory_space=pltpu.HBM)] * 7,
        out_specs=(vmem, vmem, vmem, hbm, hbm, hbm),
        scratch_shapes=[
            pltpu.VMEM(tokens.shape, BF16),
            pltpu.VMEM(tokens.shape, BF16),
            pltpu.VMEM(expert_ids.shape[::-1], jnp.int32),
            pltpu.VMEM(expert_ids.shape[::-1], F32),
            pltpu.VMEM((2 * ff, width), BF16),
            pltpu.VMEM((ff, width), BF16),
            pltpu.VMEM((2 * ff, width), BF16),
            pltpu.VMEM((ff, width), BF16),
            pltpu.VMEM((ndp, Q, LANES), F32),
            pltpu.VMEM((ndp, Q, LANES), F32),
            pltpu.VMEM((nexp, J, LANES), BF16),
            pltpu.VMEM((nexp, J, LANES), BF16),
            pltpu.VMEM((nexp, J, LANES), BF16),
            pltpu.VMEM((nexp, J, LANES), BF16),
            pltpu.VMEM((ndp, nexp // GROUP, 2, cut, ds), BF16),
            pltpu.VMEM((ndp, nexp // GROUP, 2, cut, ds), BF16),
            pltpu.VMEM((nz, nexp // GROUP, 2, cut, ds), BF16),
            pltpu.VMEM((2, far, 4, 2, cut, ds), BF16),
            pltpu.VMEM((2, far, 4, 2, cut, ds), BF16),
            pltpu.VMEM((nexp, J, LANES), BF16),
            pltpu.VMEM((nexp, J, LANES), BF16),
            pltpu.VMEM((nexp, J, LANES), BF16),
            pltpu.VMEM((nexp, J, LANES), BF16),
            pltpu.VMEM((ndp, 2 * Q, LANES), F32),
            pltpu.VMEM((ndp, 2 * Q, LANES), F32),
            pltpu.VMEM((nexp * J, ncol), BF16),
            pltpu.VMEM((nexp * J, ncol), BF16),
            pltpu.VMEM((ncol, nexp * J), BF16),
            pltpu.VMEM((ncol, nexp * J), BF16),
            pltpu.VMEM((nexp * J, ncol), F32),
            pltpu.VMEM((expert_ids.shape[1], ncol), F32),
            pltpu.VMEM((nexp, ncol), F32),
            pltpu.VMEM((nexp, ncol), F32),
            dma((4,)),
            dma((3,)),
            dma((3,)),
            dma((2,)),
            dma((2 * nexp // GROUP,)),
            dma((2 * nexp // GROUP,)),
            dma((2 * nexp // GROUP,)),
            dma((2 * nexp // GROUP,)),
            dma((2,)),
            dma((2, far, 4)),
            dma((2, far, 4)),
            dma((2, far + 1, 4)),
            dma((2, far + 1, 4)),
            dma((nz,)),
            dma((nz,)),
            dma((2, far, 4)),
            dma((2, far, 4)),
        ],
        compiler_params=pltpu.CompilerParams(
            collective_id=0, has_side_effects=True, vmem_limit_bytes=61 * 1024 * 1024
        ),
        cost_estimate=pl.CostEstimate(
            flops=18 * rows * ff * width, bytes_accessed=6 * ff * width * 2, transcendentals=rows * ff
        ),
    )(tokens, cotangent, expert_ids.T, gates.T, w_gate, w_up, w_down)
    return pl.pallas_call(
        copy_out,
        out_shape=[jax.ShapeDtypeStruct(out.shape, out.dtype) for out in outs],
        in_specs=[pl.BlockSpec(memory_space=pltpu.HBM)] * 6,
        out_specs=[pl.BlockSpec(memory_space=pltpu.HBM)] * 6,
        scratch_shapes=[pltpu.VMEM(out.shape, out.dtype) for out in outs] + [dma((3 * CHUNKS + 3,)), dma((3 * CHUNKS + 3,))],
        compiler_params=pltpu.CompilerParams(vmem_limit_bytes=61 * 1024 * 1024),
    )(*outs)


def copy_out(*refs):
    count = len(refs) // 3
    sources, targets, held = refs[:count], refs[count : 2 * count], refs[2 * count : 3 * count]
    in_sem, out_sem = refs[3 * count :]
    chunks = []
    for i in range(count)[::-1]:
        if len(sources[i].shape) == 3:
            size = sources[i].shape[1] // CHUNKS
            chunks += [(i, pl.ds(c * size, size)) for c in range(CHUNKS)]
        else:
            chunks.append((i, None))

    def move(source, target, sem, place):
        if place is None:
            return pltpu.make_async_copy(source, target, sem)
        return pltpu.make_async_copy(source.at[:, place], target.at[:, place], sem)

    gets = [move(sources[i], held[i], in_sem.at[n], p) for n, (i, p) in enumerate(chunks)]
    puts = [move(held[i], targets[i], out_sem.at[n], p) for n, (i, p) in enumerate(chunks)]
    for get in gets:
        get.start()
    for get, put in zip(gets, puts):
        get.wait()
        put.start()
    for put in puts:
        put.wait()


def solution(mesh):
    placed = (
        P(("expert", "dp"), None),
        P("expert", None),
        P("expert", None),
        P("expert", "dp", None),
        P("expert", "dp", None),
        P("expert", "dp", None),
        P(("expert", "dp"), None),
    )
    return jax.shard_map(
        on_device,
        mesh=mesh,
        in_specs=placed,
        out_specs=(
            P(("expert", "dp"), None),
            P(("expert", "dp"), None),
            P(("expert", "dp"), None),
            P("expert", "dp", None),
            P("expert", "dp", None),
            P("expert", "dp", None),
        ),
        check_vma=False,
    )
```

```python
import functools

import jax
import jax.numpy as jnp
from jax import lax
from jax.experimental import pallas as pl
from jax.experimental.pallas import tpu as pltpu
from jax.sharding import PartitionSpec as P

F32 = jnp.float32
BF16 = jnp.bfloat16
MESH = pl.DeviceIdType.MESH
SLOTS = 3
LANES = 128
Q = 8
J = 16
GROUP = 16
CHUNKS = 4
HIGH = lax.Precision.HIGHEST


def mm(left, right, left_dim=1, right_dim=0, precision=None):
    return lax.dot_general(
        left,
        right,
        (((left_dim,), (right_dim,)), ((), ())),
        preferred_element_type=F32,
        precision=precision,
    )


def iota(shape, dim):
    return lax.broadcasted_iota(jnp.int32, shape, dim)


def split2(value):
    high = value.astype(BF16)
    return high, (value - high.astype(F32)).astype(BF16)


def kernel(
    ndp,
    nexp,
    tok_hbm,
    cot_hbm,
    ids_hbm,
    gates_hbm,
    wg_ref,
    wu_ref,
    wd_ref,
    mixed_ref,
    tgrad_ref,
    ggrad_ref,
    wgg_ref,
    wug_ref,
    wdg_ref,
    tok_ref,
    cot_ref,
    ids_ref,
    gates_ref,
    wgu,
    wd,
    gu_out,
    d_out,
    send_a,
    recv_a,
    send_b,
    recv_b,
    send_f,
    recv_f,
    gath,
    part,
    sib_rx,
    ring_tx,
    ring_rx,
    send_c,
    recv_c,
    send_h,
    recv_h,
    send_d,
    recv_d,
    pd_hi,
    pd_lo,
    pr_hi,
    pr_lo,
    score_mask,
    vcol,
    slots_kept,
    weight_kept,
    i_sem,
    w_sem,
    o_sem,
    a_sem,
    b_sem,
    f_sem,
    c_sem,
    h_sem,
    d_sem,
    ag_send,
    ag_recv,
    sibg_send,
    sibg_recv,
    sibr_send,
    sibr_recv,
    rs_send,
    rs_recv,
):
    g = lax.axis_index("dp")
    e = lax.axis_index("expert")
    nz = ndp // 2
    far = nz // 2
    z = g // 2
    core = lax.rem(g, 2)
    other = 1 - core
    rows = SLOTS * nexp
    cut = SLOTS * GROUP
    parts = nexp // GROUP
    ff = wd.shape[0]
    ncol = ndp * Q
    ds = 2 * LANES
    top = ids_ref.shape[0]

    def at_z(offset, which):
        return lax.rem(z + offset + nz, nz) * 2 + which

    right = at_z(1, core)
    left = at_z(-1, core)
    sibling = z * 2 + other
    toward = (right, left)

    small = [
        pltpu.make_async_copy(tok_hbm, tok_ref, i_sem.at[0]),
        pltpu.make_async_copy(cot_hbm, cot_ref, i_sem.at[1]),
        pltpu.make_async_copy(ids_hbm, ids_ref, i_sem.at[2]),
        pltpu.make_async_copy(gates_hbm, gates_ref, i_sem.at[3]),
    ]
    for load in small:
        load.start()

    barrier = pltpu.get_barrier_semaphore()

    def greet_dp(i, carry):
        pl.semaphore_signal(
            barrier, inc=1, device_id=(lax.rem(g + i, ndp), e), device_id_type=MESH
        )
        return carry

    def greet_expert(i, carry):
        pl.semaphore_signal(
            barrier, inc=1, device_id=(g, lax.rem(e + i, nexp)), device_id_type=MESH
        )
        return carry

    lax.fori_loop(1, ndp, greet_dp, 0)
    lax.fori_loop(1, nexp, greet_expert, 0)

    loads = [
        pltpu.make_async_copy(wg_ref.at[0], wgu.at[pl.ds(0, ff)], w_sem.at[0]),
        pltpu.make_async_copy(wu_ref.at[0], wgu.at[pl.ds(ff, ff)], w_sem.at[1]),
        pltpu.make_async_copy(wd_ref.at[0], wd, w_sem.at[2]),
    ]
    for load in loads:
        load.start()

    for load in small:
        load.wait()
    token = tok_ref[...].astype(F32)
    cotan = cot_ref[...].astype(F32)
    for to in range(ndp):
        for half in range(2):
            lane = to * ds + half * LANES
            send_a[to, half : half + 1, :] = token[:, lane : lane + LANES]
            send_a[to, 2 + half : 3 + half, :] = cotan[:, lane : lane + LANES]
            send_a[(to + ndp // 2) % ndp, 4 + half : 5 + half, :] = token[:, lane : lane + LANES]
            send_a[(to + ndp // 2) % ndp, 6 + half : 7 + half, :] = cotan[:, lane : lane + LANES]

    pl.semaphore_wait(barrier, ndp - 1 + nexp - 1)

    def exchange(src, dst, sem, count, me, peer_id):
        def start(i, carry):
            peer = lax.rem(me + i, count)
            pltpu.make_async_remote_copy(
                src_ref=src.at[peer],
                dst_ref=dst.at[me],
                send_sem=sem.at[0],
                recv_sem=sem.at[1],
                device_id=peer_id(peer),
                device_id_type=MESH,
            ).start()
            return carry

        lax.fori_loop(1, count, start, 0)
        dst[me] = src[me]

    def exchange_done(src, dst, sem, count, peer_id):
        done = pltpu.make_async_remote_copy(
            src_ref=src.at[pl.ds(0, count - 1)],
            dst_ref=dst.at[pl.ds(0, count - 1)],
            send_sem=sem.at[0],
            recv_sem=sem.at[1],
            device_id=peer_id(0),
            device_id_type=MESH,
        )
        done.wait_recv()
        done.wait_send()

    def by_dp(peer):
        return (peer, e)

    def expert_start(src, dst, sem, span, way):
        def start(i, carry):
            pltpu.make_async_remote_copy(
                src_ref=src.at[i],
                dst_ref=dst.at[i],
                send_sem=sem.at[2 * span],
                recv_sem=sem.at[2 * span + 1],
                device_id=(g, lax.rem(e + way * i + nexp, nexp)),
                device_id_type=MESH,
            ).start()
            return carry

        lax.fori_loop(max(1, span * GROUP), (span + 1) * GROUP, start, 0)
        if span == 0:
            dst[0] = src[0]

    def expert_round(src, dst, sem, span):
        blocks = pl.ds(max(1, span * GROUP), (span + 1) * GROUP - max(1, span * GROUP))
        return pltpu.make_async_remote_copy(
            src_ref=src.at[blocks],
            dst_ref=dst.at[blocks],
            send_sem=sem.at[2 * span],
            recv_sem=sem.at[2 * span + 1],
            device_id=(g, e),
            device_id_type=MESH,
        )

    exchange(send_a, recv_a, a_sem, ndp, g, by_dp)

    spread_tok = (iota((ndp, ncol), 1) // Q == iota((ndp, ncol), 0)).astype(F32)
    names = mm(ids_ref[...].astype(F32), spread_tok)
    weights = mm(gates_ref[...], spread_tok, precision=HIGH)
    vcol[...] = names
    expert_row = lax.rem(iota((nexp, ncol), 0) + e, nexp).astype(F32)
    member = jnp.zeros((nexp, ncol), F32)
    weight = jnp.zeros((nexp, ncol), F32)
    for k in range(top):
        hit = names[k : k + 1, :] == expert_row
        member = jnp.where(hit, 1.0, member)
        weight = jnp.where(hit, weights[k : k + 1, :], weight)
    earlier = jnp.logical_and(
        iota((ncol, ncol), 0) // Q < iota((ncol, ncol), 1) // Q,
        lax.rem(iota((ncol, ncol), 0), Q) == 0,
    )
    rank = mm(member.astype(BF16), earlier.astype(F32).astype(BF16))
    slot_of = jnp.where(member > 0.0, rank, -1.0)
    cube = (nexp, J, ncol)
    slot3 = jnp.broadcast_to(slot_of[:, None, :], cube)
    weight3 = jnp.broadcast_to(weight[:, None, :], cube)
    jrow = iota((J, ncol), 0)
    quarter = lax.rem(iota((J, ncol), 1), Q)
    slot_j = lax.rem(jrow, SLOTS)
    used = jrow < 4 * SLOTS
    first = jrow < 2 * SLOTS
    same = jnp.logical_and(jrow // SLOTS == quarter, used)
    slot_want = jnp.where(same, slot_j, 99).astype(F32)[None]
    placed = slot3 == slot_want
    first3 = jnp.broadcast_to(first.astype(F32)[None], cube) > 0.0
    p_out = jnp.where(placed, jnp.where(first3, 1.0, weight3), 0.0).reshape(nexp * J, ncol)
    pd_hi[...], pd_lo[...] = split2(p_out)
    slots_kept[...] = slot_of
    weight_kept[...] = weight

    perm_shape = (4 * SLOTS * GROUP, GROUP * J)
    perm_row, perm_col = iota(perm_shape, 0), iota(perm_shape, 1)
    perm = jnp.logical_and(
        perm_row // GROUP == lax.rem(perm_col, J), lax.rem(perm_row, GROUP) == perm_col // J
    )
    perm = perm.astype(F32).astype(BF16)

    exchange_done(send_a, recv_a, a_sem, ndp, by_dp)
    mine = recv_a[...].reshape(ncol, LANES).astype(BF16)
    lines_of = [slice(span * GROUP * J, (span + 1) * GROUP * J) for span in range(parts)]
    for span in range(parts):
        sent = mm(pd_hi[lines_of[span]], mine) + mm(pd_lo[lines_of[span]], mine)
        send_b[span * GROUP : (span + 1) * GROUP] = sent.astype(BF16).reshape(GROUP, J, LANES)
        expert_start(send_b, recv_b, b_sem, span, 1)
    across = recv_a[...]
    across = jnp.concatenate([across[:, Q // 2 :], across[:, : Q // 2]], axis=1)
    across = across.reshape(ncol, LANES).astype(BF16)

    def send_across(span):
        sent = mm(pd_hi[lines_of[span]], across) + mm(pd_lo[lines_of[span]], across)
        send_f[span * GROUP : (span + 1) * GROUP] = sent.astype(BF16).reshape(GROUP, J, LANES)
        expert_start(send_f, recv_f, f_sem, span, 1)

    fields = [(j // (2 * SLOTS), j // SLOTS % 2, j % SLOTS) for j in range(4 * SLOTS)]

    def unpack(span, arrived, where):
        block = arrived[span * GROUP : (span + 1) * GROUP].reshape(GROUP * J, LANES)
        sorted_rows = mm(perm, block).astype(BF16)
        for j, (kind, half, slot) in enumerate(fields):
            gath[
                where,
                span,
                kind,
                slot * GROUP : (slot + 1) * GROUP,
                half * LANES : (half + 1) * LANES,
            ] = sorted_rows[j * GROUP : (j + 1) * GROUP]

    def origin(direction, step, which):
        return at_z(-step if direction == 0 else step, which)

    def goes(direction, step, piece):
        return step < far or (step == far and piece // 2 == direction)

    def ring_copy(direction, step, piece):
        spot = gath.at[origin(direction, step, core), piece]
        return pltpu.make_async_remote_copy(
            src_ref=spot,
            dst_ref=spot,
            send_sem=ag_send.at[direction, step, piece],
            recv_sem=ag_recv.at[direction, step, piece],
            device_id=(toward[direction], e),
            device_id_type=MESH,
        )

    def arrival(direction, step, piece):
        spot = gath.at[origin(direction, step + 1, core), piece]
        return pltpu.make_async_remote_copy(
            src_ref=spot,
            dst_ref=spot,
            send_sem=ag_send.at[direction, step, piece],
            recv_sem=ag_recv.at[direction, step, piece],
            device_id=(toward[direction], e),
            device_id_type=MESH,
        )

    def sib_copy(direction, step, piece, which):
        spot = gath.at[origin(direction, step, which), piece]
        return pltpu.make_async_remote_copy(
            src_ref=spot,
            dst_ref=spot,
            send_sem=sibg_send.at[direction, step, piece],
            recv_sem=sibg_recv.at[direction, step, piece],
            device_id=(sibling, e),
            device_id_type=MESH,
        )

    for piece in range(parts):
        expert_round(send_b, recv_b, b_sem, piece).wait_recv()
        unpack(piece, recv_b, g)
        for direction in range(2):
            ring_copy(direction, 0, piece).start()
        sib_copy(0, 0, piece, core).start()
        send_across(piece)

    slot3 = jnp.broadcast_to(slots_kept[...][:, None, :], cube)
    weight3 = jnp.broadcast_to(weight_kept[...][:, None, :], cube)
    placed = slot3 == slot_want
    p_back = jnp.where(placed, jnp.where(first3, weight3, 1.0), 0.0).reshape(nexp * J, ncol)
    pr_hi[...], pr_lo[...] = split2(p_back.T)
    cross = jnp.logical_and(jrow // SLOTS + 2 == quarter, first)
    cross_want = jnp.where(cross, slot_j, 99).astype(F32)[None]
    score_mask[...] = jnp.where(slot3 == cross_want, 1.0, 0.0).reshape(nexp * J, ncol)

    for step in range(1, far):
        for piece in range(4):
            for direction in range(2):
                arrival(direction, step - 1, piece).wait_recv()
                if step + 1 < far:
                    ring_copy(direction, step, piece).start()
                sib_copy(direction, step, piece, core).start()
            if step == far - 1:
                expert_round(send_f, recv_f, f_sem, piece).wait_recv()
                unpack(piece, recv_f, at_z(far, core))
                sib_copy(piece // 2, far, piece, core).start()
    for piece in range(4):
        sib_copy(0, 0, piece, other).wait_recv()
    for step in range(1, far + 1):
        for piece in range(4):
            for direction in range(2):
                if goes(direction, step, piece):
                    sib_copy(direction, step, piece, other).wait_recv()

    for load in loads:
        load.wait()

    def held(block, kind):
        return jnp.concatenate([gath[block, piece, kind] for piece in range(parts)], axis=0)

    def columns(block):
        return pl.ds(pl.multiple_of(block * ds, ds), ds)

    pre = jnp.zeros((rows, 2 * ff), F32)
    back = jnp.zeros((rows, ff), F32)
    for block in range(ndp):
        pre += mm(held(block, 0), wgu[:, block * ds : (block + 1) * ds], 1, 1)
        back += mm(held(block, 1), wd[:, block * ds : (block + 1) * ds], 1, 1)
    gate_pre = pre[:, :ff]
    up_pre = pre[:, ff:]
    logistic = 1.0 / (1.0 + jnp.exp(-gate_pre))
    silu = gate_pre * logistic
    hidden = (silu * up_pre).astype(BF16)
    act_gate = back * up_pre * logistic * (1.0 + gate_pre * (1.0 - logistic))
    act_up = back * silu
    acts = jnp.concatenate([act_gate, act_up], axis=1).astype(BF16)

    def make_part(block):
        outs = (
            mm(hidden, wd[:, columns(block)]).astype(BF16),
            mm(acts, wgu[:, columns(block)]).astype(BF16),
        )
        for piece in range(parts):
            for kind in range(2):
                part[block, piece, kind] = outs[kind][piece * cut : (piece + 1) * cut]

    def pair_copy(place, which):
        return pltpu.make_async_remote_copy(
            src_ref=part.at[at_z(place, which)],
            dst_ref=sib_rx.at[at_z(place, 0) // 2],
            send_sem=sibr_send.at[place],
            recv_sem=sibr_recv.at[place],
            device_id=(sibling, e),
            device_id_type=MESH,
        )

    def make_parts(places):
        for place in places:
            make_part(at_z(place, other))
            pair_copy(place, other).start()
            make_part(at_z(place, core))

    def at_distance(away):
        return sorted({away, (nz - away) % nz})

    make_parts(at_distance(far - 1))

    def chain_copy(direction, step, piece):
        return pltpu.make_async_remote_copy(
            src_ref=ring_tx.at[direction, step, piece],
            dst_ref=ring_rx.at[direction, step, piece],
            send_sem=rs_send.at[direction, step, piece],
            recv_sem=rs_recv.at[direction, step, piece],
            device_id=(toward[direction], e),
            device_id_type=MESH,
        )

    def chip_sum(place, piece):
        return part[at_z(place, core), piece].astype(F32) + sib_rx[
            at_z(place, 0) // 2, piece
        ].astype(F32)

    def weight_grads(blocks):
        for block in blocks:
            cols = slice(block * ds, (block + 1) * ds)
            gu_out[:, cols] = mm(acts, held(block, 0), 0, 0).astype(BF16)
            d_out[:, cols] = mm(hidden, held(block, 1), 0, 0).astype(BF16)

    unperm_shape = (GROUP * J, 4 * SLOTS * GROUP)
    un_row, un_col = iota(unperm_shape, 0), iota(unperm_shape, 1)
    unperm = jnp.logical_and(
        un_col // GROUP == lax.rem(un_row, J), lax.rem(un_col, GROUP) == un_row // J
    )
    unperm = unperm.astype(F32).astype(BF16)

    def send_home(total, src, dst, sem, piece):
        final = total.astype(BF16)
        taken = [
            final[kind, slot * GROUP : (slot + 1) * GROUP, half * LANES : (half + 1) * LANES]
            for kind, half, slot in fields
        ]
        block = mm(unperm, jnp.concatenate(taken, axis=0)).astype(BF16)
        src[piece * GROUP : (piece + 1) * GROUP] = block.reshape(GROUP, J, LANES)
        expert_start(src, dst, sem, piece, -1)

    turns = [(step, piece) for step in range(1, far) for piece in range(4)]
    paired = set()
    done_blocks = 0
    for turn, (step, piece) in enumerate(turns):
        for direction in range(2):
            away = far - step
            place = away if direction == 0 else nz - away
            if place not in paired:
                pair_copy(place, other).wait_recv()
                paired.add(place)
            total = chip_sum(place, piece)
            if step > 1:
                chain_copy(direction, step - 1, piece).wait_recv()
                total += ring_rx[direction, step - 1, piece].astype(F32)
            ring_tx[direction, step, piece] = total.astype(BF16)
            chain_copy(direction, step, piece).start()
        if turn == 1:
            make_parts(at_distance(far))
        elif turn == 3:
            make_parts(at_distance(far - 2))
        elif 4 <= turn < 8:
            if turn == 4:
                pair_copy(far, other).wait_recv()
            send_home(chip_sum(far, turn - 4), send_h, recv_h, h_sem, turn - 4)
            if turn == 5:
                make_parts(at_distance(far - 3))
            if turn == 7:
                make_parts(at_distance(0))
        elif turn >= 8:
            weight_grads(range(done_blocks, min(ndp, done_blocks + 4)))
            done_blocks = min(ndp, done_blocks + 4)
    weight_grads(range(done_blocks, ndp))
    stores = [
        pltpu.make_async_copy(gu_out.at[pl.ds(0, ff)], wgg_ref.at[0], o_sem.at[0]),
        pltpu.make_async_copy(gu_out.at[pl.ds(ff, ff)], wug_ref.at[0], o_sem.at[1]),
        pltpu.make_async_copy(d_out, wdg_ref.at[0], o_sem.at[2]),
    ]
    for store in stores:
        store.start()
    pair_copy(0, other).wait_recv()
    for piece in range(parts):
        total = chip_sum(0, piece)
        for direction in range(2):
            chain_copy(direction, far - 1, piece).wait_recv()
            total += ring_rx[direction, far - 1, piece].astype(F32)
        send_home(total, send_c, recv_c, c_sem, piece)

    result = jnp.zeros((ncol, LANES), F32)
    mine = recv_a[...].reshape(ncol, LANES).astype(BF16)
    result_far = jnp.zeros((ncol, LANES), F32)
    across = recv_a[...]
    across = jnp.concatenate([across[:, Q // 2 :], across[:, : Q // 2]], axis=1)
    across = across.reshape(ncol, LANES).astype(BF16)
    by_span = []
    for span in range(parts):
        expert_round(send_h, recv_h, h_sem, span).wait_recv()
        came = recv_h[span * GROUP : (span + 1) * GROUP].reshape(GROUP * J, LANES)
        lines = lines_of[span]
        result_far += mm(pr_hi[:, lines], came) + mm(pr_lo[:, lines], came)
        products = mm(came, across, 1, 1) * score_mask[lines]
        by_span.append(jnp.sum(products.reshape(GROUP, J, ncol), axis=1))
    far_scores = jnp.concatenate(by_span, axis=0)
    by_span = []
    for span in range(parts):
        expert_round(send_c, recv_c, c_sem, span).wait_recv()
        came = recv_c[span * GROUP : (span + 1) * GROUP].reshape(GROUP * J, LANES)
        lines = lines_of[span]
        result += mm(pr_hi[:, lines], came) + mm(pr_lo[:, lines], came)
        products = mm(came, mine, 1, 1) * score_mask[lines]
        by_span.append(jnp.sum(products.reshape(GROUP, J, ncol), axis=1))
    per_expert = jnp.concatenate(by_span, axis=0) + far_scores
    names = vcol[...]
    expert_row = lax.rem(iota((nexp, ncol), 0) + e, nexp).astype(F32)
    scores = [
        jnp.sum(jnp.where(names[k : k + 1, :] == expert_row, per_expert, 0.0), axis=0, keepdims=True)
        for k in range(top)
    ]
    scores = jnp.concatenate(scores + [jnp.zeros((LANES - top, ncol), F32)], axis=0)
    pick = jnp.logical_and(
        iota((ncol, ncol), 0) // Q == iota((ncol, ncol), 1) // Q,
        lax.rem(iota((ncol, ncol), 0), Q) == 0,
    ).astype(F32)
    result_far = result_far.reshape(ndp, Q, LANES)
    result_far = jnp.concatenate([result_far[:, Q // 2 :], result_far[:, : Q // 2]], axis=1)
    send_d[:, :Q] = result.reshape(ndp, Q, LANES) + result_far
    send_d[:, Q:] = mm(pick, scores, 1, 1, HIGH).reshape(ndp, Q, LANES)
    exchange(send_d, recv_d, d_sem, ndp, g, by_dp)
    exchange_done(send_d, recv_d, d_sem, ndp, by_dp)
    out_cols, grad_cols = [], []
    total = jnp.zeros((1, LANES), F32)
    for came_from in range(ndp):
        for half in range(2):
            facing = (came_from + ndp // 2) % ndp
            out_cols.append(
                recv_d[came_from, half : half + 1, :] + recv_d[facing, 4 + half : 5 + half, :]
            )
            grad_cols.append(
                recv_d[came_from, 2 + half : 3 + half, :] + recv_d[facing, 6 + half : 7 + half, :]
            )
        total += recv_d[came_from, Q : Q + 1, :]
    mixed_ref[...] = jnp.concatenate(out_cols, axis=1).astype(BF16)
    tgrad_ref[...] = jnp.concatenate(grad_cols, axis=1).astype(BF16)
    ggrad_ref[...] = total[:, :top]

    for span in range(parts):
        expert_round(send_b, recv_b, b_sem, span).wait_send()
        expert_round(send_f, recv_f, f_sem, span).wait_send()
        expert_round(send_c, recv_c, c_sem, span).wait_send()
        expert_round(send_h, recv_h, h_sem, span).wait_send()
    for piece in range(4):
        sib_copy(0, 0, piece, core).wait_send()
    for step in range(far + 1):
        for piece in range(4):
            for direction in range(2):
                if step < far - 1:
                    ring_copy(direction, step, piece).wait_send()
                if step > 0 and goes(direction, step, piece):
                    sib_copy(direction, step, piece, core).wait_send()
                if 0 < step < far:
                    chain_copy(direction, step, piece).wait_send()
    for place in range(nz):
        pair_copy(place, other).wait_send()
    for store in stores:
        store.wait()


def on_device(tokens, expert_ids, gates, w_gate, w_up, w_down, cotangent):
    ndp, nexp = lax.axis_size("dp"), lax.axis_size("expert")
    nz, far = ndp // 2, ndp // 4
    ff, width = w_down.shape[1:]
    rows = SLOTS * nexp
    cut, ds, ncol = SLOTS * GROUP, 2 * LANES, ndp * Q
    vmem, hbm = pl.BlockSpec(memory_space=pltpu.VMEM), pl.BlockSpec(memory_space=pl.ANY)
    row = jax.ShapeDtypeStruct(tokens.shape, BF16)
    weight = jax.ShapeDtypeStruct(w_down.shape, BF16)
    dma = pltpu.SemaphoreType.DMA
    outs = pl.pallas_call(
        functools.partial(kernel, ndp, nexp),
        out_shape=(
            row,
            row,
            jax.ShapeDtypeStruct((1, expert_ids.shape[1]), F32),
            weight,
            weight,
            weight,
        ),
        in_specs=[pl.BlockSpec(memory_space=pltpu.HBM)] * 7,
        out_specs=(vmem, vmem, vmem, hbm, hbm, hbm),
        scratch_shapes=[
            pltpu.VMEM(tokens.shape, BF16),
            pltpu.VMEM(tokens.shape, BF16),
            pltpu.VMEM(expert_ids.shape[::-1], jnp.int32),
            pltpu.VMEM(expert_ids.shape[::-1], F32),
            pltpu.VMEM((2 * ff, width), BF16),
            pltpu.VMEM((ff, width), BF16),
            pltpu.VMEM((2 * ff, width), BF16),
            pltpu.VMEM((ff, width), BF16),
            pltpu.VMEM((ndp, Q, LANES), F32),
            pltpu.VMEM((ndp, Q, LANES), F32),
            pltpu.VMEM((nexp, J, LANES), BF16),
            pltpu.VMEM((nexp, J, LANES), BF16),
            pltpu.VMEM((nexp, J, LANES), BF16),
            pltpu.VMEM((nexp, J, LANES), BF16),
            pltpu.VMEM((ndp, nexp // GROUP, 2, cut, ds), BF16),
            pltpu.VMEM((ndp, nexp // GROUP, 2, cut, ds), BF16),
            pltpu.VMEM((nz, nexp // GROUP, 2, cut, ds), BF16),
            pltpu.VMEM((2, far, 4, 2, cut, ds), BF16),
            pltpu.VMEM((2, far, 4, 2, cut, ds), BF16),
            pltpu.VMEM((nexp, J, LANES), BF16),
            pltpu.VMEM((nexp, J, LANES), BF16),
            pltpu.VMEM((nexp, J, LANES), BF16),
            pltpu.VMEM((nexp, J, LANES), BF16),
            pltpu.VMEM((ndp, 2 * Q, LANES), F32),
            pltpu.VMEM((ndp, 2 * Q, LANES), F32),
            pltpu.VMEM((nexp * J, ncol), BF16),
            pltpu.VMEM((nexp * J, ncol), BF16),
            pltpu.VMEM((ncol, nexp * J), BF16),
            pltpu.VMEM((ncol, nexp * J), BF16),
            pltpu.VMEM((nexp * J, ncol), F32),
            pltpu.VMEM((expert_ids.shape[1], ncol), F32),
            pltpu.VMEM((nexp, ncol), F32),
            pltpu.VMEM((nexp, ncol), F32),
            dma((4,)),
            dma((3,)),
            dma((3,)),
            dma((2,)),
            dma((2 * nexp // GROUP,)),
            dma((2 * nexp // GROUP,)),
            dma((2 * nexp // GROUP,)),
            dma((2 * nexp // GROUP,)),
            dma((2,)),
            dma((2, far, 4)),
            dma((2, far, 4)),
            dma((2, far + 1, 4)),
            dma((2, far + 1, 4)),
            dma((nz,)),
            dma((nz,)),
            dma((2, far, 4)),
            dma((2, far, 4)),
        ],
        compiler_params=pltpu.CompilerParams(
            collective_id=0, has_side_effects=True, vmem_limit_bytes=61 * 1024 * 1024
        ),
        cost_estimate=pl.CostEstimate(
            flops=18 * rows * ff * width, bytes_accessed=6 * ff * width * 2, transcendentals=rows * ff
        ),
    )(tokens, cotangent, expert_ids.T, gates.T, w_gate, w_up, w_down)
    return pl.pallas_call(
        copy_out,
        out_shape=[jax.ShapeDtypeStruct(out.shape, out.dtype) for out in outs],
        in_specs=[pl.BlockSpec(memory_space=pltpu.HBM)] * 6,
        out_specs=[pl.BlockSpec(memory_space=pltpu.HBM)] * 6,
        scratch_shapes=[pltpu.VMEM(out.shape, out.dtype) for out in outs] + [dma((3 * CHUNKS + 3,)), dma((3 * CHUNKS + 3,))],
        compiler_params=pltpu.CompilerParams(vmem_limit_bytes=61 * 1024 * 1024),
    )(*outs)


def copy_out(*refs):
    count = len(refs) // 3
    sources, targets, held = refs[:count], refs[count : 2 * count], refs[2 * count : 3 * count]
    in_sem, out_sem = refs[3 * count :]
    chunks = []
    for i in range(count)[::-1]:
        if len(sources[i].shape) == 3:
            size = sources[i].shape[1] // CHUNKS
            chunks += [(i, pl.ds(c * size, size)) for c in range(CHUNKS)]
        else:
            chunks.append((i, None))

    def move(source, target, sem, place):
        if place is None:
            return pltpu.make_async_copy(source, target, sem)
        return pltpu.make_async_copy(source.at[:, place], target.at[:, place], sem)

    gets = [move(sources[i], held[i], in_sem.at[n], p) for n, (i, p) in enumerate(chunks)]
    puts = [move(held[i], targets[i], out_sem.at[n], p) for n, (i, p) in enumerate(chunks)]
    for get in gets:
        get.start()
    for get, put in zip(gets, puts):
        get.wait()
        put.start()
    for put in puts:
        put.wait()


def solution(mesh):
    placed = (
        P(("expert", "dp"), None),
        P("expert", None),
        P("expert", None),
        P("expert", "dp", None),
        P("expert", "dp", None),
        P("expert", "dp", None),
        P(("expert", "dp"), None),
    )
    return jax.shard_map(
        on_device,
        mesh=mesh,
        in_specs=placed,
        out_specs=(
            P(("expert", "dp"), None),
            P(("expert", "dp"), None),
            P(("expert", "dp"), None),
            P("expert", "dp", None),
            P("expert", "dp", None),
            P("expert", "dp", None),
        ),
        check_vma=False,
    )
```
